512 devices in a mesh: chan: 128 (over y, x_lo, z), win: 4 (over x_hi, core).
Axes of the slice: x: 4 (x_hi: 2, x_lo: 2; x = x_hi * 2 + x_lo), y: 8, z: 8, core: 2. Of those that a mesh axis runs over, the one named last changes fastest.
Arguments:
- spectra: bfloat16 [4096, 16, 2, 4096], P('chan', 'win'), may hold values from -500 to 500
- pair_list: int32 [12288, 3], P('chan'), may hold values from 0 to 4095, as said below
- quality: int32 [4096], P('chan'), may hold values 0 or 1
Outputs:
- stacked: float32 [12288, 1024], P('chan', 'win')
The draws below stay inside these ranges and needn't reach their ends.
Inputs may be any that keep to these rules, and one draw needn't show every extreme that they name: `pair_list`: row i belongs to channel block b = i // 96 (channels b * 32 to b * 32 + 31). Column 0 is a source channel of that block, column 1 a receiver channel at most 64 channels from the source, column 2 is 1 for a used pair and 0 otherwise. In every draw used pairs reach that distance on both sides in every block whose neighbours lie on the fibre.
All inputs are finite; a program needn't handle non-finite values. No bound on the sum of `quality` on one device may be relied on, other than what follows from the above.
Results may differ from the reference program's by a relative error of at most 0.015.
Values may be sent and summed in bfloat16 or wider, within the bound.
A program may use at most 64 MiB of HBM per device.

```python
import math
import jax
import jax.numpy as jnp
from jax import lax

CH_DEV = 32
P_CAP = 96
NF = 4096
LAGS = 1024
WB = 64
HB = 2
CHANNELS = 4096
NSUB = 16
PAIRS = 12288
N_CHAN = 128


def draw_spectra(key, part):
    key = jax.random.fold_in(key, 5)
    key_base, key_chan, key_band = jax.random.split(key, 3)
    band_count = NF // WB
    base = jnp.clip(jax.random.normal(key_base, (CHANNELS, NSUB, 2, band_count, WB), jnp.float32), -5.0, 5.0)
    chan_scale = jnp.exp(jax.random.uniform(key_chan, (CHANNELS, 1, 1, 1, 1), jnp.float32, 0.0, math.log(10.0)))
    band_scale = jnp.exp(jax.random.uniform(key_band, (CHANNELS, NSUB, 1, band_count, 1), jnp.float32, 0.0, math.log(10.0)))
    return (base * chan_scale * band_scale).reshape(CHANNELS, NSUB, 2, NF).astype(jnp.bfloat16)


def draw_pair_list(key, part):
    key = jax.random.fold_in(key, 11)
    key_src, key_off, key_keep = jax.random.split(key, 3)
    reach = HB * CH_DEV
    slot_index = jnp.arange(PAIRS, dtype=jnp.int32)
    block_index = slot_index // P_CAP
    within = slot_index % P_CAP
    source = block_index * CH_DEV + jax.random.randint(key_src, (PAIRS,), 0, CH_DEV, dtype=jnp.int32)
    offset = jax.random.randint(key_off, (PAIRS,), -reach, reach + 1, dtype=jnp.int32)
    offset = jnp.where(within == 0, -reach, jnp.where(within == 1, reach, offset))
    raw_receiver = source + offset
    inside = (raw_receiver >= 0) & (raw_receiver < CHANNELS)
    kept = (jax.random.randint(key_keep, (PAIRS,), 0, 8, dtype=jnp.int32) < 7) | (within < 2)
    in_use = (inside & kept).astype(jnp.int32)
    receiver = jnp.clip(raw_receiver, 0, CHANNELS - 1)
    return jnp.stack([source, receiver, in_use], axis=1)


def touch_ends(drawn, own_key, low, largest):
    shape = drawn.shape
    index_at = [jax.random.randint(jax.random.fold_in(own_key, axis), (), 0, shape[axis]) for axis in range(len(shape))]
    drawn = drawn.at[tuple(index_at)].set(low)
    longest = shape.index(max(shape))
    index_at[longest] = (index_at[longest] + 1) % shape[longest]
    return drawn.at[tuple(index_at)].set(largest)


def setup_inputs(seed: int = 0) -> dict:
    key_of = jax.random.split(jax.random.key(seed), 4)
    spectra = draw_spectra(jax.random.fold_in(key_of[3], 71), 0)
    pair_list = draw_pair_list(jax.random.fold_in(key_of[3], 71), 0)
    quality = touch_ends((jax.random.randint(key_of[2], (CHANNELS,), 0, 8) < 7).astype(jnp.int32), jax.random.fold_in(key_of[2], 1), 0, 1)
    return {"spectra": spectra, "pair_list": pair_list, "quality": quality}


tiny_level = 1e-06

def whiten(spectra, quality):
    chan_count = spectra.shape[0]
    sub_count = spectra.shape[1]
    bin_count = spectra.shape[3]
    values = spectra.astype(jnp.float32)
    magnitude = jnp.sqrt(values[:, :, 0] * values[:, :, 0] + values[:, :, 1] * values[:, :, 1])
    band_level = magnitude.reshape(chan_count, sub_count, bin_count // WB, WB).mean(axis=-1)
    factor = quality.astype(jnp.float32)[:, None, None, None, None] / (band_level[:, :, None, :, None] + tiny_level)
    shaped = values.reshape(chan_count, sub_count, 2, bin_count // WB, WB) * factor
    return shaped.reshape(spectra.shape).astype(jnp.bfloat16)

def lag_tables(first_bin, bin_total):
    frequency = first_bin + jnp.arange(bin_total, dtype=jnp.int32)
    lag_index = jnp.arange(LAGS, dtype=jnp.int32) - LAGS // 2
    phase_index = jnp.mod(frequency[:, None] * lag_index[None, :], 2 * NF)
    radians = phase_index.astype(jnp.float32) * (math.pi / NF)
    table_scale = 1.0 / math.sqrt(NF)
    return ((jnp.cos(radians) * table_scale).astype(jnp.bfloat16), (jnp.sin(radians) * table_scale).astype(jnp.bfloat16))

def cross_lags(src_rows, rcv_rows, in_use, cos_table, sin_table):
    source = src_rows.astype(jnp.float32)
    receiver = rcv_rows.astype(jnp.float32)
    src_re = source[:, :, 0]
    src_im = source[:, :, 1]
    rcv_re = receiver[:, :, 0]
    rcv_im = receiver[:, :, 1]
    real_part = (src_re * rcv_re + src_im * rcv_im) * in_use[:, None, None]
    imag_part = (src_im * rcv_re - src_re * rcv_im) * in_use[:, None, None]
    row_count = real_part.shape[0] * real_part.shape[1]
    real_rows = real_part.astype(jnp.bfloat16).reshape(row_count, real_part.shape[2])
    imag_rows = imag_part.astype(jnp.bfloat16).reshape(row_count, real_part.shape[2])
    return jnp.dot(real_rows, cos_table, preferred_element_type=jnp.float32) - jnp.dot(imag_rows, sin_table, preferred_element_type=jnp.float32)

def reference(spectra, pair_list, quality):
    whitened = whiten(spectra, quality)
    cos_table, sin_table = lag_tables(0, NF)
    blocks = pair_list.reshape(N_CHAN, P_CAP, 3)

    def one_block(block_pairs):
        src_rows = jnp.take(whitened, block_pairs[:, 0].astype(jnp.int32), axis=0)
        rcv_rows = jnp.take(whitened, block_pairs[:, 1].astype(jnp.int32), axis=0)
        in_use = block_pairs[:, 2].astype(jnp.float32)
        lagged = cross_lags(src_rows, rcv_rows, in_use, cos_table, sin_table)
        return lagged.reshape(P_CAP, NSUB, LAGS).sum(axis=1) * (1.0 / math.sqrt(NSUB))
    return lax.map(one_block, blocks).reshape(PAIRS, LAGS)
```

```python
import functools
import math

import jax
import jax.numpy as jnp
import numpy as np
import ml_dtypes
from jax import lax
from jax.experimental import pallas as pl
from jax.experimental.pallas import tpu as pltpu
from jax.sharding import PartitionSpec as P

MESH = pl.DeviceIdType.MESH
NF = 4096
LAGS = 1024
WB = 64
LANES = 128
tiny_level = 1e-06

RUNS = 8
PART = RUNS * LANES
PARTS = NF // PART


def lag_tables(groups):
    frequency = np.arange(NF, dtype=np.int64)
    lag_index = np.arange(LAGS, dtype=np.int64) - LAGS // 2
    phase = np.mod(frequency[:, None] * lag_index[None, :], 2 * NF)
    angle = np.arange(2 * NF, dtype=np.float64) * (math.pi / NF)
    scale = 1.0 / math.sqrt(NF)
    cos_of = (np.cos(angle) * scale).astype(ml_dtypes.bfloat16)
    sin_of = (-np.sin(angle) * scale).astype(ml_dtypes.bfloat16)
    both = np.stack([cos_of[phase], sin_of[phase]])
    both = both.reshape(2, PARTS, RUNS, LANES, groups, LAGS // groups)
    both = both.transpose(1, 4, 2, 0, 3, 5)
    return both.reshape(PARTS, groups, RUNS * 2 * LANES, LAGS // groups)


def band_mean():
    lane = np.arange(LANES)
    return ((lane[:, None] // WB == lane[None, :] // WB) / WB).astype(ml_dtypes.bfloat16)


def kernel(
    chan_total, quality, spectra, pairs, pairs_out, mean_of, table,
    out,
    near0, near1, near2, near3, loose, cross, sums, tab, pair_in, pair_near, src_at, rcv_at,
    core_out, core_in, home_out, home_in, half_out, half_in,
    part_send, part_recv, pair_send, pair_recv, pair_local, tab_sem, tail_send, tail_recv,
):
    near = (near0, near1, near2, near3)
    chan = lax.axis_index("chan")
    win = lax.axis_index("win")
    chans = spectra.shape[0]
    subs = spectra.shape[1]
    slots = pairs.shape[1]
    rows = 3 * slots
    wide = LAGS // 4
    core = lax.rem(win, 2)
    x_hi = win // 2
    right = (lax.rem(chan + 1, chan_total), win)
    left = (lax.rem(chan + chan_total - 1, chan_total), win)
    mate = (chan, win + 1 - 2 * core)
    across = (chan, lax.rem(win + 2, 4))

    tables = []
    for part in range(PARTS):
        for g in range(4):
            group = (g % 2) * 2 + (1 - core if g < 2 else core)
            copy = pltpu.make_async_copy(table.at[part, group], tab.at[part, g], tab_sem.at[part, g])
            copy.start()
            tables.append(copy)

    barrier = pltpu.get_barrier_semaphore()
    for peer in (left, right, mate, across):
        pl.semaphore_signal(barrier, inc=1, device_id=peer, device_id_type=MESH)
    pl.semaphore_wait(barrier, 4)

    pair_copies = []
    for side, peer in ((0, right), (1, left)):
        copy = pltpu.make_async_remote_copy(
            src_ref=pairs_out, dst_ref=pair_in.at[side],
            send_sem=pair_send.at[side], recv_sem=pair_recv.at[side],
            device_id=peer, device_id_type=MESH,
        )
        copy.start()
        pair_copies.append(copy)

    def whiten(part):
        step = 4

        def some(i, carry):
            first = i * step
            block = spectra[pl.ds(first, step), :, pl.ds(part * 2 * RUNS, 2 * RUNS), :]
            count = step * subs * RUNS
            loose[...] = block.astype(jnp.float32).reshape(2 * count, LANES)
            real = loose[pl.ds(0, count, stride=2), :]
            imag = loose[pl.ds(1, count, stride=2), :]
            magnitude = jnp.sqrt(real * real + imag * imag)
            level = jnp.dot(magnitude.astype(jnp.bfloat16), mean_of[...], preferred_element_type=jnp.float32)
            weight = 1.0 / (level + tiny_level)
            real = (real * weight).reshape(step, subs * RUNS, LANES)
            imag = (imag * weight).reshape(step, subs * RUNS, LANES)
            for j in range(step):
                good = quality[first + j].astype(jnp.float32)
                near[part][chans + first + j, 0 : subs * RUNS, :] = (real[j] * good).astype(jnp.bfloat16)
                near[part][chans + first + j, subs * RUNS :, :] = (imag[j] * good).astype(jnp.bfloat16)
            return carry

        lax.fori_loop(0, chans // step, some, 0)
        near[part][3 * chans] = jnp.zeros(near[part].shape[1:], jnp.bfloat16)

    part_copies = []
    for part in range(PARTS):
        whiten(part)
        copies = []
        for side, peer in ((0, right), (1, left)):
            copy = pltpu.make_async_remote_copy(
                src_ref=near[part].at[pl.ds(chans, chans)],
                dst_ref=near[part].at[pl.ds(2 * chans * side, chans)],
                send_sem=part_send.at[part, side], recv_sem=part_recv.at[part, side],
                device_id=peer, device_id_type=MESH,
            )
            copy.start()
            copies.append(copy)
        part_copies.append(copies)

    for copy in pair_copies:
        copy.wait()
    local = pltpu.make_async_copy(pair_in, pair_near, pair_local)
    local.start()
    local.wait()

    empty = 3 * chans
    base = (chan - 1) * chans

    def place(p, carry):
        def put(row, source, receiver, used, low, high):
            at = receiver - base
            fits = (used != 0) & (at >= low) & (at < high)
            src_at[row] = jnp.where(fits, source - base, empty)
            rcv_at[row] = jnp.where(fits, at, empty)

        put(p, pairs[0, p], pairs[1, p], pairs[2, p], 0, 3 * chans)
        has_left = (chan > 0).astype(jnp.int32)
        has_right = (chan < chan_total - 1).astype(jnp.int32)
        put(
            slots + p, pair_near[0, 0, p], pair_near[0, 1, p], pair_near[0, 2, p] * has_left,
            2 * chans, 2 * chans + chans * has_right,
        )
        put(
            2 * slots + p, pair_near[1, 0, p], pair_near[1, 1, p], pair_near[1, 2, p] * has_right,
            0, chans * has_left,
        )
        return carry

    lax.fori_loop(0, slots, place, 0)

    half = subs * RUNS

    def products(part):
        here = near[part]
        unroll = 4

        def some(i, carry):
            for j in range(unroll):
                p = i * unroll + j
                a = here[src_at[p]]
                b = here[rcv_at[p]]
                real = a[:half] * b[:half] + a[half:] * b[half:]
                imag = a[half:] * b[:half] - a[:half] * b[half:]
                real = real.astype(jnp.float32).reshape(subs, RUNS, LANES).sum(axis=0)
                imag = imag.astype(jnp.float32).reshape(subs, RUNS, LANES).sum(axis=0)
                cross[pl.ds(p, RUNS, stride=2 * rows), :] = real
                cross[pl.ds(p + rows, RUNS, stride=2 * rows), :] = imag
            return carry

        lax.fori_loop(0, rows // unroll, some, 0)

    def lags(part, g):
        wide_rows = jnp.concatenate(
            [cross[pl.ds(k * rows, rows), :].astype(jnp.bfloat16) for k in range(2 * RUNS)], axis=1
        )
        return jnp.dot(wide_rows, tab[part, g], preferred_element_type=jnp.float32)

    for copy in tables:
        copy.wait()

    def remote(src, dst, which, peer):
        copy = pltpu.make_async_remote_copy(
            src_ref=src, dst_ref=dst, send_sem=tail_send.at[which], recv_sem=tail_recv.at[which],
            device_id=peer, device_id_type=MESH,
        )
        copy.start()
        return copy

    tail = []
    for part in range(PARTS):
        for copy in part_copies[part]:
            copy.wait()
        products(part)
        for g in range(4):
            total = lags(part, g)
            if part > 0:
                total = total + sums[g]
            if part < PARTS - 1 or g >= 2:
                sums[g] = total
            else:
                core_out[g] = total.astype(jnp.bfloat16)
                tail.append(remote(core_out.at[g], core_in.at[g], g, mate))

    for g in range(2):
        tail[g].wait()
        both = sums[2 + g] + core_in[g].astype(jnp.float32)
        sums[2 + g] = both
        for side in range(2):
            home_out[side, g] = both[(1 + side) * slots : (2 + side) * slots].astype(jnp.bfloat16)
    back = [remote(home_out.at[0], home_in.at[1], 2, left), remote(home_out.at[1], home_in.at[0], 3, right)]
    for copy in back:
        copy.wait()

    def home_sum(g):
        return (
            sums[2 + g, 0:slots, :]
            + home_in[0, g].astype(jnp.float32)
            + home_in[1, g].astype(jnp.float32)
        )

    half_out[...] = home_sum(1 - x_hi).astype(jnp.bfloat16)
    last = remote(half_out, half_in, 4, across)
    mine = home_sum(x_hi)
    last.wait()
    out[...] = (mine + half_in[...].astype(jnp.float32)) * (1.0 / math.sqrt(subs * 4))


def on_device(chan_total, spectra, pair_list, quality):
    chans, subs = spectra.shape[0], spectra.shape[1]
    slots = pair_list.shape[0]
    rows = 3 * slots
    runs = NF // LANES
    tiles = spectra.reshape(chans, subs, 2, runs, LANES).transpose(0, 1, 3, 2, 4)
    tiles = tiles.reshape(chans, subs, 2 * runs, LANES)
    pairs = pair_list.T
    table = jnp.asarray(lag_tables(4))
    vmem = pl.BlockSpec(memory_space=pltpu.VMEM)
    smem = pl.BlockSpec(memory_space=pltpu.SMEM)
    wide = LAGS // 4
    near = pltpu.VMEM((3 * chans + 1, 2 * subs * RUNS, LANES), jnp.bfloat16)
    sem = pltpu.SemaphoreType.DMA
    return pl.pallas_call(
        functools.partial(kernel, chan_total),
        out_shape=jax.ShapeDtypeStruct((slots, wide), jnp.float32),
        in_specs=[smem, vmem, smem, vmem, vmem, pl.BlockSpec(memory_space=pl.ANY)],
        out_specs=vmem,
        scratch_shapes=[
            near, near, near, near,
            pltpu.VMEM((4 * subs * RUNS * 2, LANES), jnp.float32),
            pltpu.VMEM((2 * RUNS * rows, LANES), jnp.float32),
            pltpu.VMEM((4, rows, wide), jnp.float32),
            pltpu.VMEM((PARTS, 4, 2 * PART, wide), jnp.bfloat16),
            pltpu.VMEM((2,) + pairs.shape, jnp.int32),
            pltpu.SMEM((2,) + pairs.shape, jnp.int32),
            pltpu.SMEM((rows,), jnp.int32),
            pltpu.SMEM((rows,), jnp.int32),
            pltpu.VMEM((2, rows, wide), jnp.bfloat16),
            pltpu.VMEM((2, rows, wide), jnp.bfloat16),
            pltpu.VMEM((2, 2, slots, wide), jnp.bfloat16),
            pltpu.VMEM((2, 2, slots, wide), jnp.bfloat16),
            pltpu.VMEM((slots, wide), jnp.bfloat16),
            pltpu.VMEM((slots, wide), jnp.bfloat16),
            sem((PARTS, 2)), sem((PARTS, 2)), sem((2,)), sem((2,)), sem, sem((PARTS, 4)), sem((5,)), sem((5,)),
        ],
        compiler_params=pltpu.CompilerParams(
            collective_id=0, has_side_effects=True, vmem_limit_bytes=56 * 1024 * 1024
        ),
    )(quality, tiles, pairs, pairs, jnp.asarray(band_mean()), table)


def solution(mesh):
    return jax.shard_map(
        functools.partial(on_device, mesh.shape["chan"]),
        mesh=mesh,
        in_specs=(P("chan", "win", None, None), P("chan", None), P("chan")),
        out_specs=P("chan", "win"),
        check_vma=False,
    )
```

```python
import functools
import math

import jax
import jax.numpy as jnp
import numpy as np
import ml_dtypes
from jax import lax
from jax.experimental import pallas as pl
from jax.experimental.pallas import tpu as pltpu
from jax.sharding import PartitionSpec as P

MESH = pl.DeviceIdType.MESH
NF = 4096
LAGS = 1024
WB = 64
LANES = 128
tiny_level = 1e-06

RUNS = 8
GROUPS = NF // (RUNS * LANES)
PARTS = ((0, 0, 8), (1, 0, 8), (2, 0, 8), (3, 0, 4), (3, 4, 4))
WINS = 4
WIDE = LAGS // WINS


def lag_tables():
    frequency = np.arange(NF, dtype=np.int64)
    lag_index = np.arange(LAGS, dtype=np.int64) - LAGS // 2
    phase = np.mod(frequency[:, None] * lag_index[None, :], 2 * NF)
    angle = np.arange(2 * NF, dtype=np.float64) * (math.pi / NF)
    scale = 1.0 / math.sqrt(NF)
    cos_of = (np.cos(angle) * scale).astype(ml_dtypes.bfloat16)
    sin_of = (-np.sin(angle) * scale).astype(ml_dtypes.bfloat16)
    both = np.stack([cos_of[phase], sin_of[phase]])
    both = both.reshape(2, GROUPS, RUNS, LANES, WINS, WIDE)
    both = both.transpose(1, 4, 2, 0, 3, 5)
    return both.reshape(GROUPS, WINS, RUNS * 2 * LANES, WIDE)


def band_mean():
    lane = np.arange(LANES)
    return ((lane[:, None] // WB == lane[None, :] // WB) / WB).astype(ml_dtypes.bfloat16)


def kernel(
    chan_total, quality, pairs, pairs_out, mean_of, spectra, table,
    out,
    near0, near1, near2, near3, near4, fresh, loose, cross, left_rows, sums, tab,
    pair_in, pair_near, src_at, rcv_at,
    core_out, core_in, home_out, home_in, own_out, own_in,
    fresh_sem, tab_sem, part_send, part_recv, pair_send, pair_recv, pair_local, tail_send, tail_recv,
):
    near = (near0, near1, near2, near3, near4)
    chan = lax.axis_index("chan")
    win = lax.axis_index("win")
    chans = quality.shape[0]
    subs = spectra.shape[1]
    slots = pairs.shape[1]
    rows = 3 * slots
    core = lax.rem(win, 2)
    x_hi = win // 2
    has_left = (chan > 0).astype(jnp.int32)
    has_right = (chan < chan_total - 1).astype(jnp.int32)
    win_mate = x_hi * 2 + 1 - core
    win_across = (1 - x_hi) * 2 + core
    win_cross = (1 - x_hi) * 2 + 1 - core

    barrier = pltpu.get_barrier_semaphore()

    def greet(peer):
        pl.semaphore_signal(barrier, inc=1, device_id=peer, device_id_type=MESH)

    @pl.when(chan > 0)
    def _():
        greet((chan - 1, win))
        greet((chan - 1, win_across))

    @pl.when(chan < chan_total - 1)
    def _():
        greet((chan + 1, win))
        greet((chan + 1, win_across))

    greet((chan, win_mate))
    greet((chan, win_across))
    greet((chan, win_cross))

    fetched = []
    for group in range(GROUPS):
        copy = pltpu.make_async_copy(
            spectra.at[:, :, pl.ds(group * 2 * RUNS, 2 * RUNS), :], fresh.at[group], fresh_sem.at[group]
        )
        copy.start()
        fetched.append(copy)
    @pl.when(chan == 0)
    def _():
        for part in range(len(PARTS)):
            near[part][0:chans] = jnp.zeros((chans,) + near[part].shape[1:], jnp.bfloat16)
        pair_in[0] = jnp.zeros(pair_in.shape[1:], jnp.int32)
        home_in[0] = jnp.zeros(home_in.shape[1:], jnp.bfloat16)

    @pl.when(chan == chan_total - 1)
    def _():
        for part in range(len(PARTS)):
            near[part][2 * chans : 3 * chans] = jnp.zeros((chans,) + near[part].shape[1:], jnp.bfloat16)
        pair_in[1] = jnp.zeros(pair_in.shape[1:], jnp.int32)
        home_in[1] = jnp.zeros(home_in.shape[1:], jnp.bfloat16)

    def whiten(group):
        step = 4
        mine = [(p, first, runs) for p, (g, first, runs) in enumerate(PARTS) if g == group]
        fetched[group].wait()

        def some(i, carry):
            start = i * step
            block = fresh[group, pl.ds(start, step)]
            count = step * subs * RUNS
            loose[...] = block.astype(jnp.float32).reshape(2 * count, LANES)
            real = loose[pl.ds(0, count, stride=2), :]
            imag = loose[pl.ds(1, count, stride=2), :]
            magnitude = jnp.sqrt(real * real + imag * imag)
            level = jnp.dot(magnitude.astype(jnp.bfloat16), mean_of[...], preferred_element_type=jnp.float32)
            weight = 1.0 / (level + tiny_level)
            real = (real * weight).reshape(step, subs, RUNS, LANES)
            imag = (imag * weight).reshape(step, subs, RUNS, LANES)
            for j in range(step):
                good = quality[start + j].astype(jnp.float32)
                for p, first, runs in mine:
                    half = subs * runs
                    for k, values in ((0, real), (1, imag)):
                        kept = (values[j, :, first : first + runs] * good).reshape(half, LANES)
                        near[p][chans + start + j, k * half : (k + 1) * half, :] = kept.astype(jnp.bfloat16)
            return carry

        lax.fori_loop(0, chans // step, some, 0)
        for p, first, runs in mine:
            near[p][3 * chans] = jnp.zeros(near[p].shape[1:], jnp.bfloat16)

    def both_ways(to_right, to_left):
        @pl.when(chan < chan_total - 1)
        def _():
            to_right.start()

        @pl.when(chan > 0)
        def _():
            to_left.start()

    def both_waits(to_right, to_left):
        @pl.when(chan < chan_total - 1)
        def _():
            to_right.wait_send()
            to_left.wait_recv()

        @pl.when(chan > 0)
        def _():
            to_left.wait_send()
            to_right.wait_recv()

    def beside(src, dsts, send, recv):
        return [
            pltpu.make_async_remote_copy(
                src_ref=src, dst_ref=dsts[side], send_sem=send.at[side], recv_sem=recv.at[side],
                device_id=(peer, win), device_id_type=MESH,
            )
            for side, peer in ((0, chan + 1), (1, chan - 1))
        ]

    whiten(0)
    pl.semaphore_wait(barrier, 3 + 2 * has_left + 2 * has_right)

    pair_copies = beside(pairs_out, [pair_in.at[0], pair_in.at[1]], pair_send, pair_recv)
    part_copies = []
    for group in range(GROUPS):
        if group > 0:
            whiten(group)
        for p, (g, first, runs) in enumerate(PARTS):
            if g == group:
                copies = beside(
                    near[p].at[pl.ds(chans, chans)],
                    [near[p].at[pl.ds(0, chans)], near[p].at[pl.ds(2 * chans, chans)]],
                    part_send.at[p], part_recv.at[p],
                )
                both_ways(*copies)
                part_copies.append(copies)
        if group == 0:
            both_ways(*pair_copies)

    tables = []
    for group in range(GROUPS):
        for g, quarter in enumerate((win_cross, win_mate, win_across, win)):
            copy = pltpu.make_async_copy(table.at[group, quarter], tab.at[group, g], tab_sem.at[group, g])
            copy.start()
            tables.append(copy)

    both_waits(*pair_copies)
    local = pltpu.make_async_copy(pair_in, pair_near, pair_local)
    local.start()
    local.wait()

    empty = 3 * chans
    base = (chan - 1) * chans

    def place(p, carry):
        def put(row, source, receiver, used, low, high):
            at = receiver - base
            fits = (used != 0) & (at >= low) & (at < high)
            src_at[row] = jnp.where(fits, source - base, empty)
            rcv_at[row] = jnp.where(fits, at, empty)

        put(p, pairs[0, p], pairs[1, p], pairs[2, p], 0, 3 * chans)
        between = has_left * has_right
        put(
            slots + p, pair_near[0, 0, p], pair_near[0, 1, p], pair_near[0, 2, p] * between,
            2 * chans, 3 * chans,
        )
        put(
            2 * slots + p, pair_near[1, 0, p], pair_near[1, 1, p], pair_near[1, 2, p] * between,
            0, chans,
        )
        return carry

    lax.fori_loop(0, slots, place, 0)

    def products(part, low, high):
        runs = PARTS[part][2]
        half = subs * runs
        here = near[part]
        unroll = 4

        def fold(values):
            values = values.astype(jnp.float32).reshape(half // 8, 8, LANES).sum(axis=0)
            if runs == 4:
                values = values[:4] + values[4:]
            return values

        def some(i, carry):
            for j in range(unroll):
                p = low + i * unroll + j
                a = here[src_at[p]]
                b = here[rcv_at[p]]
                real = a[:half] * b[:half] + a[half:] * b[half:]
                imag = a[half:] * b[:half] - a[:half] * b[half:]
                cross[pl.ds(p, runs, stride=2 * rows), :] = fold(real)
                cross[pl.ds(p + rows, runs, stride=2 * rows), :] = fold(imag)
            return carry

        lax.fori_loop(0, (high - low) // unroll, some, 0)
        for k in range(2 * runs):
            left_rows[low:high, k * LANES : (k + 1) * LANES] = cross[k * rows + low : k * rows + high, :].astype(
                jnp.bfloat16
            )

    def lags(part, low, high, g):
        group, first, runs = PARTS[part]
        depth = 2 * runs * LANES
        return jnp.dot(
            left_rows[low:high, :depth], tab[group, g, 2 * first * LANES : 2 * first * LANES + depth, :],
            preferred_element_type=jnp.float32,
        )

    for copy in tables:
        copy.wait()

    for part in range(len(PARTS) - 1):
        both_waits(*part_copies[part])
        products(part, 0, rows)
        for g in range(WINS):
            total = lags(part, 0, rows, g)
            sums[g] = total if part == 0 else total + sums[g]

    def remote(src, dst, which, peer):
        return pltpu.make_async_remote_copy(
            src_ref=src, dst_ref=dst, send_sem=tail_send.at[which], recv_sem=tail_recv.at[which],
            device_id=peer, device_id_type=MESH,
        )

    part = len(PARTS) - 1
    both_waits(*part_copies[part])
    products(part, slots, rows)
    core_copies = []
    for g in range(2):
        core_out[g] = (lags(part, slots, rows, g) + sums[g, slots:rows]).astype(jnp.bfloat16)
        copy = remote(core_out.at[g], core_in.at[g], g, (chan, win_mate))
        copy.start()
        core_copies.append(copy)
    home_copies = []
    ahead = [lags(part, slots, rows, 2 + g) + sums[2 + g, slots:rows] for g in range(2)]
    for g, to_win in ((0, win_across), (1, win)):
        core_copies[g].wait()
        home_out[g] = (ahead[g] + core_in[g].astype(jnp.float32)).astype(jnp.bfloat16)
        copies = [
            remote(home_out.at[g, pl.ds(slots, slots)], home_in.at[0, g], 2 + 2 * g, (chan + 1, to_win)),
            remote(home_out.at[g, pl.ds(0, slots)], home_in.at[1, g], 3 + 2 * g, (chan - 1, to_win)),
        ]
        both_ways(*copies)
        home_copies.append(copies)

    products(part, 0, slots)
    own_copies = []
    for g, to_win in ((0, win_cross), (1, win_mate), (2, win_across)):
        own_out[g] = (lags(part, 0, slots, g) + sums[g, 0:slots]).astype(jnp.bfloat16)
        copy = remote(own_out.at[g], own_in.at[g], 6 + g, (chan, to_win))
        copy.start()
        own_copies.append(copy)
    total = lags(part, 0, slots, 3) + sums[3, 0:slots]
    for copy in own_copies:
        copy.wait()
    for g in range(3):
        total = total + own_in[g].astype(jnp.float32)
    for copies in home_copies:
        both_waits(*copies)
    for g in range(2):
        total = total + home_in[0, g].astype(jnp.float32) + home_in[1, g].astype(jnp.float32)
    out[...] = total * (1.0 / math.sqrt(subs * WINS))


def on_device(chan_total, spectra, pair_list, quality):
    chans, subs = spectra.shape[0], spectra.shape[1]
    slots = pair_list.shape[0]
    rows = 3 * slots
    runs = NF // LANES
    tiles = spectra.reshape(chans, subs, 2, runs, LANES).transpose(0, 1, 3, 2, 4)
    tiles = tiles.reshape(chans, subs, 2 * runs, LANES)
    pairs = pair_list.T
    vmem = pl.BlockSpec(memory_space=pltpu.VMEM)
    smem = pl.BlockSpec(memory_space=pltpu.SMEM)
    anywhere = pl.BlockSpec(memory_space=pl.ANY)
    sem = pltpu.SemaphoreType.DMA
    bf16 = jnp.bfloat16
    return pl.pallas_call(
        functools.partial(kernel, chan_total),
        out_shape=jax.ShapeDtypeStruct((slots, WIDE), jnp.float32),
        in_specs=[smem, smem, vmem, vmem, anywhere, anywhere],
        out_specs=vmem,
        scratch_shapes=[pltpu.VMEM((3 * chans + 1, 2 * subs * part[2], LANES), bf16) for part in PARTS]
        + [
            pltpu.VMEM((GROUPS, chans, subs, 2 * RUNS, LANES), bf16),
            pltpu.VMEM((4 * subs * RUNS * 2, LANES), jnp.float32),
            pltpu.VMEM((2 * RUNS * rows, LANES), jnp.float32),
            pltpu.VMEM((rows, 2 * RUNS * LANES), bf16),
            pltpu.VMEM((WINS, rows, WIDE), jnp.float32),
            pltpu.VMEM((GROUPS, WINS, 2 * RUNS * LANES, WIDE), bf16),
            pltpu.VMEM((2,) + pairs.shape, jnp.int32),
            pltpu.SMEM((2,) + pairs.shape, jnp.int32),
            pltpu.SMEM((rows,), jnp.int32),
            pltpu.SMEM((rows,), jnp.int32),
            pltpu.VMEM((2, 2 * slots, WIDE), bf16),
            pltpu.VMEM((2, 2 * slots, WIDE), bf16),
            pltpu.VMEM((2, 2 * slots, WIDE), bf16),
            pltpu.VMEM((2, 2, slots, WIDE), bf16),
            pltpu.VMEM((3, slots, WIDE), bf16),
            pltpu.VMEM((3, slots, WIDE), bf16),
            sem((GROUPS,)), sem((GROUPS, WINS)), sem((len(PARTS), 2)), sem((len(PARTS), 2)),
            sem((2,)), sem((2,)), sem, sem((9,)), sem((9,)),
        ],
        compiler_params=pltpu.CompilerParams(
            collective_id=0, has_side_effects=True, vmem_limit_bytes=56 * 1024 * 1024
        ),
    )(quality, pairs, pairs, jnp.asarray(band_mean()), tiles, jnp.asarray(lag_tables()))


def solution(mesh):
    return jax.shard_map(
        functools.partial(on_device, mesh.shape["chan"]),
        mesh=mesh,
        in_specs=(P("chan", "win", None, None), P("chan", None), P("chan")),
        out_specs=P("chan", "win"),
        check_vma=False,
    )
```

```python
import functools
import math

import jax
import jax.numpy as jnp
import numpy as np
import ml_dtypes
from jax import lax
from jax.experimental import pallas as pl
from jax.experimental.pallas import tpu as pltpu
from jax.sharding import PartitionSpec as P

MESH = pl.DeviceIdType.MESH
NF = 4096
LAGS = 1024
WB = 64
LANES = 128
tiny_level = 1e-06

RUNS = 8
GROUPS = NF // (RUNS * LANES)
PARTS = ((0, 0, 8), (1, 0, 8), (2, 0, 8), (3, 0, 4), (3, 4, 4))
WINS = 4
WIDE = LAGS // WINS


def lag_tables():
    frequency = np.arange(NF, dtype=np.int64)
    lag_index = np.arange(LAGS, dtype=np.int64) - LAGS // 2
    phase = np.mod(frequency[:, None] * lag_index[None, :], 2 * NF)
    angle = np.arange(2 * NF, dtype=np.float64) * (math.pi / NF)
    scale = 1.0 / math.sqrt(NF)
    cos_of = (np.cos(angle) * scale).astype(ml_dtypes.bfloat16)
    sin_of = (-np.sin(angle) * scale).astype(ml_dtypes.bfloat16)
    both = np.stack([cos_of[phase], sin_of[phase]])
    both = both.reshape(2, GROUPS, RUNS, LANES, WINS, WIDE)
    both = both.transpose(1, 4, 2, 0, 3, 5)
    return both.reshape(GROUPS, WINS, RUNS * 2 * LANES, WIDE)


def band_mean():
    here = lax.broadcasted_iota(jnp.int32, (LANES, LANES), 0) // WB
    there = lax.broadcasted_iota(jnp.int32, (LANES, LANES), 1) // WB
    return jnp.where(here == there, 1.0 / WB, 0.0).astype(jnp.bfloat16)


def kernel(
    chan_total, quality_in, pairs_out, spectra, table,
    out,
    near0, near1, near2, near3, near4, fresh, loose, cross, left_rows, sums, tab,
    quality, pairs, pair_in, pair_near, src_at, rcv_at,
    core_out, core_in, home_out, home_in, own_out, own_in,
    small_sem, fresh_sem, tab_sem, part_send, part_recv, pair_send, pair_recv, pair_local, tail_send, tail_recv,
):
    near = (near0, near1, near2, near3, near4)
    chan = lax.axis_index("chan")
    win = lax.axis_index("win")
    chans = spectra.shape[0]
    subs = spectra.shape[1]
    slots = pairs.shape[1]
    rows = 3 * slots
    pitch = rows + 8
    core = lax.rem(win, 2)
    x_hi = win // 2
    has_left = (chan > 0).astype(jnp.int32)
    has_right = (chan < chan_total - 1).astype(jnp.int32)
    win_mate = x_hi * 2 + 1 - core
    win_across = (1 - x_hi) * 2 + core
    win_cross = (1 - x_hi) * 2 + 1 - core

    barrier = pltpu.get_barrier_semaphore()

    def greet(peer):
        pl.semaphore_signal(barrier, inc=1, device_id=peer, device_id_type=MESH)

    @pl.when(chan > 0)
    def _():
        greet((chan - 1, win))
        greet((chan - 1, win_across))

    @pl.when(chan < chan_total - 1)
    def _():
        greet((chan + 1, win))
        greet((chan + 1, win_across))

    greet((chan, win_mate))
    greet((chan, win_across))
    greet((chan, win_cross))

    small = [
        pltpu.make_async_copy(src, dst, small_sem.at[i])
        for i, (src, dst) in enumerate(((quality_in, quality), (pairs_out, pairs)))
    ]
    for copy in small:
        copy.start()
    fetched = []
    for group in range(GROUPS):
        copy = pltpu.make_async_copy(
            spectra.at[:, :, pl.ds(group * 2 * RUNS, 2 * RUNS), :], fresh.at[group], fresh_sem.at[group]
        )
        copy.start()
        fetched.append(copy)
    @pl.when(chan == 0)
    def _():
        for part in range(len(PARTS)):
            near[part][0:chans] = jnp.zeros((chans,) + near[part].shape[1:], jnp.bfloat16)
        pair_in[0] = jnp.zeros(pair_in.shape[1:], jnp.int32)
        home_in[0] = jnp.zeros(home_in.shape[1:], jnp.bfloat16)

    @pl.when(chan == chan_total - 1)
    def _():
        for part in range(len(PARTS)):
            near[part][2 * chans : 3 * chans] = jnp.zeros((chans,) + near[part].shape[1:], jnp.bfloat16)
        pair_in[1] = jnp.zeros(pair_in.shape[1:], jnp.int32)
        home_in[1] = jnp.zeros(home_in.shape[1:], jnp.bfloat16)

    def whiten(group):
        step = 4
        mine = [(p, first, runs) for p, (g, first, runs) in enumerate(PARTS) if g == group]
        fetched[group].wait()

        def some(i, carry):
            start = i * step
            block = fresh[group, pl.ds(start, step)]
            count = step * subs * RUNS
            loose[...] = block.astype(jnp.float32).reshape(2 * count, LANES)
            real = loose[pl.ds(0, count, stride=2), :]
            imag = loose[pl.ds(1, count, stride=2), :]
            magnitude = jnp.sqrt(real * real + imag * imag)
            level = jnp.dot(magnitude.astype(jnp.bfloat16), mean_of, preferred_element_type=jnp.float32)
            weight = 1.0 / (level + tiny_level)
            real = (real * weight).reshape(step, subs, RUNS, LANES)
            imag = (imag * weight).reshape(step, subs, RUNS, LANES)
            for j in range(step):
                good = quality[start + j].astype(jnp.float32)
                for p, first, runs in mine:
                    half = subs * runs
                    for k, values in ((0, real), (1, imag)):
                        kept = (values[j, :, first : first + runs] * good).reshape(half, LANES)
                        near[p][chans + start + j, k * half : (k + 1) * half, :] = kept.astype(jnp.bfloat16)
            return carry

        lax.fori_loop(0, chans // step, some, 0)
        for p, first, runs in mine:
            near[p][3 * chans] = jnp.zeros(near[p].shape[1:], jnp.bfloat16)

    def both_ways(to_right, to_left):
        @pl.when(chan < chan_total - 1)
        def _():
            to_right.start()

        @pl.when(chan > 0)
        def _():
            to_left.start()

    def both_land(to_right, to_left):
        @pl.when(chan > 0)
        def _():
            to_right.wait_recv()

        @pl.when(chan < chan_total - 1)
        def _():
            to_left.wait_recv()

    def both_sent(to_right, to_left):
        @pl.when(chan < chan_total - 1)
        def _():
            to_right.wait_send()

        @pl.when(chan > 0)
        def _():
            to_left.wait_send()

    def beside(src, dsts, send, recv):
        return [
            pltpu.make_async_remote_copy(
                src_ref=src, dst_ref=dsts[side], send_sem=send.at[side], recv_sem=recv.at[side],
                device_id=(peer, win), device_id_type=MESH,
            )
            for side, peer in ((0, chan + 1), (1, chan - 1))
        ]

    mean_of = band_mean()
    for copy in small:
        copy.wait()
    whiten(0)
    pl.semaphore_wait(barrier, 3 + 2 * has_left + 2 * has_right)

    pair_copies = beside(pairs_out, [pair_in.at[0], pair_in.at[1]], pair_send, pair_recv)
    part_copies = []
    for group in range(GROUPS):
        if group > 0:
            whiten(group)
        for p, (g, first, runs) in enumerate(PARTS):
            if g == group:
                copies = beside(
                    near[p].at[pl.ds(chans, chans)],
                    [near[p].at[pl.ds(0, chans)], near[p].at[pl.ds(2 * chans, chans)]],
                    part_send.at[p], part_recv.at[p],
                )
                both_ways(*copies)
                part_copies.append(copies)
        if group == 0:
            both_ways(*pair_copies)

    tables = []
    for group in range(GROUPS):
        for g, quarter in enumerate((win_cross, win_mate, win_across, win)):
            copy = pltpu.make_async_copy(table.at[group, quarter], tab.at[group, g], tab_sem.at[group, g])
            copy.start()
            tables.append(copy)

    both_land(*pair_copies)
    local = pltpu.make_async_copy(pair_in, pair_near, pair_local)
    local.start()
    local.wait()

    empty = 3 * chans
    base = (chan - 1) * chans

    def place(p, carry):
        def put(row, source, receiver, used, low, high):
            at = receiver - base
            fits = (used != 0) & (at >= low) & (at < high)
            src_at[row] = jnp.where(fits, source - base, empty)
            rcv_at[row] = jnp.where(fits, at, empty)

        put(p, pairs[0, p], pairs[1, p], pairs[2, p], 0, 3 * chans)
        between = has_left * has_right
        put(
            slots + p, pair_near[0, 0, p], pair_near[0, 1, p], pair_near[0, 2, p] * between,
            2 * chans, 3 * chans,
        )
        put(
            2 * slots + p, pair_near[1, 0, p], pair_near[1, 1, p], pair_near[1, 2, p] * between,
            0, chans,
        )
        return carry

    lax.fori_loop(0, slots, place, 0)

    def products(part, low, high):
        runs = PARTS[part][2]
        half = subs * runs
        here = near[part]
        unroll = 16

        def fold(values):
            values = values.astype(jnp.float32).reshape(half // 8, 8, LANES).sum(axis=0)
            if runs == 4:
                values = values[:4] + values[4:]
            return values

        def some(i, carry):
            for j in range(unroll):
                p = low + i * unroll + j
                a = here[src_at[p]]
                b = here[rcv_at[p]]
                real = a[:half] * b[:half] + a[half:] * b[half:]
                imag = a[half:] * b[:half] - a[:half] * b[half:]
                cross[pl.ds(p, runs, stride=pitch), :] = fold(real)
                cross[pl.ds(p + RUNS * pitch, runs, stride=pitch), :] = fold(imag)
            return carry

        lax.fori_loop(0, (high - low) // unroll, some, 0)
        for k in range(2 * runs):
            left_rows[low:high, k * LANES : (k + 1) * LANES] = cross[((k % 2) * RUNS + k // 2) * pitch + low : ((k % 2) * RUNS + k // 2) * pitch + high, :].astype(
                jnp.bfloat16
            )

    def lags(part, low, high, g):
        group, first, runs = PARTS[part]
        depth = 2 * runs * LANES
        return jnp.dot(
            left_rows[low:high, :depth], tab[group, g, 2 * first * LANES : 2 * first * LANES + depth, :],
            preferred_element_type=jnp.float32,
        )

    for copy in tables:
        copy.wait()

    for part in range(len(PARTS) - 1):
        both_land(*part_copies[part])
        products(part, 0, rows)
        for g in range(WINS):
            total = lags(part, 0, rows, g)
            sums[g] = total if part == 0 else total + sums[g]

    def remote(src, dst, which, peer):
        return pltpu.make_async_remote_copy(
            src_ref=src, dst_ref=dst, send_sem=tail_send.at[which], recv_sem=tail_recv.at[which],
            device_id=peer, device_id_type=MESH,
        )

    part = len(PARTS) - 1
    both_land(*part_copies[part])
    sides = ((0, 2 * slots), (1, slots))

    def to_mate(side, low):
        for g in range(2):
            core_out[side, g] = (lags(part, low, low + slots, g) + sums[g, low : low + slots]).astype(jnp.bfloat16)
        copy = remote(core_out.at[side], core_in.at[side], side, (chan, win_mate))
        copy.start()
        return copy

    def to_home(side, ahead, core_copy):
        core_copy.wait_recv()
        copies = []
        for g, to_win in ((0, win_across), (1, win)):
            home_out[side, g] = (ahead[g] + core_in[side, g].astype(jnp.float32)).astype(jnp.bfloat16)
            copies.append(
                remote(home_out.at[side, g], home_in.at[side, g], 2 + 2 * side + g, (chan + 1 - 2 * side, to_win))
            )

        @pl.when(chan < chan_total - 1 if side == 0 else chan > 0)
        def _():
            for copy in copies:
                copy.start()

        return copies

    def kept(low, g):
        return lags(part, low, low + slots, g) + sums[g, low : low + slots]

    (_, right_low), (_, left_low) = sides
    products(part, right_low, right_low + slots)
    core_right = to_mate(0, right_low)
    ahead = [kept(right_low, 2), kept(right_low, 3)]
    products(part, left_low, left_low + slots)
    home_right = to_home(0, ahead, core_right)
    core_left = to_mate(1, left_low)
    ahead = [kept(left_low, 2), kept(left_low, 3)]

    products(part, 0, slots)
    home_left = to_home(1, ahead, core_left)
    own_copies = []
    for g, to_win in ((0, win_cross), (2, win_across), (1, win_mate)):
        own_out[g] = kept(0, g).astype(jnp.bfloat16)
        copy = remote(own_out.at[g], own_in.at[g], 6 + g, (chan, to_win))
        copy.start()
        own_copies.append(copy)
    total = kept(0, 3)

    for copies in part_copies:
        both_sent(*copies)
    both_sent(*pair_copies)
    core_right.wait_send()
    core_left.wait_send()
    for copy in own_copies:
        copy.wait()
    for g in range(3):
        total = total + own_in[g].astype(jnp.float32)
    for to_left in home_left:
        @pl.when(chan < chan_total - 1)
        def _():
            to_left.wait_recv()

        @pl.when(chan > 0)
        def _():
            to_left.wait_send()

    for g in range(2):
        total = total + home_in[1, g].astype(jnp.float32)
    for to_right in home_right:
        @pl.when(chan < chan_total - 1)
        def _():
            to_right.wait_send()

        @pl.when(chan > 0)
        def _():
            to_right.wait_recv()

    for g in range(2):
        total = total + home_in[0, g].astype(jnp.float32)
    out[...] = total


def on_device(chan_total, spectra, pair_list, quality):
    chans, subs = spectra.shape[0], spectra.shape[1]
    slots = pair_list.shape[0]
    rows = 3 * slots
    runs = NF // LANES
    tiles = spectra.reshape(chans, subs, 2, runs, LANES).transpose(0, 1, 3, 2, 4)
    tiles = tiles.reshape(chans, subs, 2 * runs, LANES)
    pairs = pair_list.T
    hbm = pl.BlockSpec(memory_space=pltpu.HBM)
    sem = pltpu.SemaphoreType.DMA
    bf16 = jnp.bfloat16
    total = pl.pallas_call(
        functools.partial(kernel, chan_total),
        out_shape=pltpu.VMEM((slots, WIDE), jnp.float32),
        in_specs=[hbm] * 4,
        out_specs=pl.BlockSpec(memory_space=pltpu.VMEM),
        scratch_shapes=[pltpu.VMEM((3 * chans + 1, 2 * subs * part[2], LANES), bf16) for part in PARTS]
        + [
            pltpu.VMEM((GROUPS, chans, subs, 2 * RUNS, LANES), bf16),
            pltpu.VMEM((4 * subs * RUNS * 2, LANES), jnp.float32),
            pltpu.VMEM((2 * RUNS * (rows + 8), LANES), jnp.float32),
            pltpu.VMEM((rows, 2 * RUNS * LANES), bf16),
            pltpu.VMEM((WINS, rows, WIDE), jnp.float32),
            pltpu.VMEM((GROUPS, WINS, 2 * RUNS * LANES, WIDE), bf16),
            pltpu.SMEM(quality.shape, jnp.int32),
            pltpu.SMEM(pairs.shape, jnp.int32),
            pltpu.VMEM((2,) + pairs.shape, jnp.int32),
            pltpu.SMEM((2,) + pairs.shape, jnp.int32),
            pltpu.SMEM((rows,), jnp.int32),
            pltpu.SMEM((rows,), jnp.int32),
            pltpu.VMEM((2, 2, slots, WIDE), bf16),
            pltpu.VMEM((2, 2, slots, WIDE), bf16),
            pltpu.VMEM((2, 2, slots, WIDE), bf16),
            pltpu.VMEM((2, 2, slots, WIDE), bf16),
            pltpu.VMEM((3, slots, WIDE), bf16),
            pltpu.VMEM((3, slots, WIDE), bf16),
            sem((2,)), sem((GROUPS,)), sem((GROUPS, WINS)), sem((len(PARTS), 2)), sem((len(PARTS), 2)),
            sem((2,)), sem((2,)), sem, sem((9,)), sem((9,)),
        ],
        compiler_params=pltpu.CompilerParams(
            collective_id=0, has_side_effects=True, vmem_limit_bytes=63 * 1024 * 1024
        ),
    )(quality, pairs, tiles, jnp.asarray(lag_tables()))
    return total * (1.0 / math.sqrt(subs * WINS))


def solution(mesh):
    return jax.shard_map(
        functools.partial(on_device, mesh.shape["chan"]),
        mesh=mesh,
        in_specs=(P("chan", "win", None, None), P("chan", None), P("chan")),
        out_specs=P("chan", "win"),
        check_vma=False,
    )
```

```python
import functools
import math

import jax
import jax.numpy as jnp
import numpy as np
import ml_dtypes
from jax import lax
from jax.experimental import pallas as pl
from jax.experimental.pallas import tpu as pltpu
from jax.sharding import PartitionSpec as P

MESH = pl.DeviceIdType.MESH
NF = 4096
LAGS = 1024
WB = 64
LANES = 128
tiny_level = 1e-06

RUNS = 8
GROUPS = NF // (RUNS * LANES)
PARTS = ((0, 0, 8), (1, 0, 8), (2, 0, 8), (3, 0, 4), (3, 4, 2), (3, 6, 2))
LAST, EXTRA = 4, 5
TO_RIGHT = (0, 1, 2, EXTRA, 3, LAST)
TO_LEFT = (0, 1, 2, 3, LAST, EXTRA)
WINS = 4
WIDE = LAGS // WINS


def lag_tables():
    frequency = np.arange(NF, dtype=np.int64)
    lag_index = np.arange(LAGS, dtype=np.int64) - LAGS // 2
    phase = np.mod(frequency[:, None] * lag_index[None, :], 2 * NF)
    angle = np.arange(2 * NF, dtype=np.float64) * (math.pi / NF)
    scale = 1.0 / math.sqrt(NF)
    cos_of = (np.cos(angle) * scale).astype(ml_dtypes.bfloat16)
    sin_of = (-np.sin(angle) * scale).astype(ml_dtypes.bfloat16)
    both = np.stack([cos_of[phase], sin_of[phase]])
    both = both.reshape(2, GROUPS, RUNS, LANES, WINS, WIDE)
    both = both.transpose(1, 4, 2, 0, 3, 5)
    return both.reshape(GROUPS, WINS, RUNS * 2 * LANES, WIDE)


def band_mean():
    here = lax.broadcasted_iota(jnp.int32, (LANES, LANES), 0) // WB
    there = lax.broadcasted_iota(jnp.int32, (LANES, LANES), 1) // WB
    return jnp.where(here == there, 1.0 / WB, 0.0).astype(jnp.bfloat16)


def kernel(
    chan_total, quality_in, pairs_out, spectra, table,
    out,
    near0, near1, near2, near3, near4, near5, beyond, fresh, loose, cross, left_rows, sums, tab,
    quality, pairs, pair_in, pair_near, src_at, rcv_at, far_src_at, far_rcv_at, beyond_at,
    core_out, core_in, home_out, home_in, own_out, own_in,
    small_sem, fresh_sem, tab_sem, part_send, part_recv, far_send, far_recv, pair_send, pair_recv, pair_local, tail_send, tail_recv,
):
    near = (near0, near1, near2, near3, near4, near5)
    chan = lax.axis_index("chan")
    win = lax.axis_index("win")
    chans = spectra.shape[0]
    subs = spectra.shape[1]
    slots = pairs.shape[1]
    rows = 3 * slots
    pitch = rows + 8
    core = lax.rem(win, 2)
    x_hi = win // 2
    has_left = (chan > 0).astype(jnp.int32)
    has_right = (chan < chan_total - 1).astype(jnp.int32)
    win_mate = x_hi * 2 + 1 - core
    win_across = (1 - x_hi) * 2 + core
    win_cross = (1 - x_hi) * 2 + 1 - core

    barrier = pltpu.get_barrier_semaphore()

    def greet(peer):
        pl.semaphore_signal(barrier, inc=1, device_id=peer, device_id_type=MESH)

    @pl.when(chan < chan_total - 1)
    def _():
        greet((chan + 1, win))
        greet((chan + 1, win_across))

    @pl.when(chan > 0)
    def _():
        greet((chan - 1, win))
        greet((chan - 1, win_across))

    greet((chan, win_mate))
    greet((chan, win_across))
    greet((chan, win_cross))

    small = [
        pltpu.make_async_copy(src, dst, small_sem.at[i])
        for i, (src, dst) in enumerate(((quality_in, quality), (pairs_out, pairs)))
    ]
    for copy in small:
        copy.start()
    halves = [(0, chans // 2), (chans // 2, chans)]
    fetched = []
    for group in range(GROUPS):
        pieces = halves if group == 0 else [(0, chans)]
        copies = []
        for n, (low, high) in enumerate(pieces):
            copy = pltpu.make_async_copy(
                spectra.at[pl.ds(low, high - low), :, pl.ds(group * 2 * RUNS, 2 * RUNS), :],
                fresh.at[group, pl.ds(low, high - low)], fresh_sem.at[group, n],
            )
            copy.start()
            copies.append(copy)
        fetched.append(copies)
    @pl.when(chan == 0)
    def _():
        for part in range(len(PARTS)):
            near[part][0:chans] = jnp.zeros((chans,) + near[part].shape[1:], jnp.bfloat16)
        pair_in[0] = jnp.zeros(pair_in.shape[1:], jnp.int32)
        home_in[0] = jnp.zeros(home_in.shape[1:], jnp.bfloat16)

    beyond[chans] = jnp.zeros(beyond.shape[1:], jnp.bfloat16)

    @pl.when(chan < 2)
    def _():
        beyond[0:chans] = jnp.zeros((chans,) + beyond.shape[1:], jnp.bfloat16)

    @pl.when(chan == chan_total - 1)
    def _():
        for part in range(len(PARTS)):
            near[part][2 * chans : 3 * chans] = jnp.zeros((chans,) + near[part].shape[1:], jnp.bfloat16)
        pair_in[1] = jnp.zeros(pair_in.shape[1:], jnp.int32)
        home_in[1] = jnp.zeros(home_in.shape[1:], jnp.bfloat16)

    def whiten(group, low, high):
        step = 4
        mine = [(p, first, runs) for p, (g, first, runs) in enumerate(PARTS) if g == group]
        def some(i, carry):
            start = low + i * step
            block = fresh[group, pl.ds(start, step)]
            count = step * subs * RUNS
            loose[0 : 2 * count] = block.astype(jnp.float32).reshape(2 * count, LANES)
            real = loose[pl.ds(0, count, stride=2), :]
            imag = loose[pl.ds(1, count, stride=2), :]
            magnitude = jnp.sqrt(real * real + imag * imag)
            level = jnp.dot(magnitude.astype(jnp.bfloat16), mean_of, preferred_element_type=jnp.float32)
            weight = 1.0 / (level + tiny_level)
            real = (real * weight).reshape(step, subs, RUNS, LANES)
            imag = (imag * weight).reshape(step, subs, RUNS, LANES)
            for j in range(step):
                good = quality[start + j].astype(jnp.float32)
                for p, first, runs in mine:
                    kept = [
                        (values[j, :, first : first + runs] * good).reshape(subs * runs, LANES)
                        for values in (real, imag)
                    ]
                    near[p][chans + start + j] = jnp.concatenate(kept, axis=0).astype(jnp.bfloat16)
            return carry

        lax.fori_loop(0, (high - low) // step, some, 0)
        for p, first, runs in mine:
            near[p][3 * chans] = jnp.zeros(near[p].shape[1:], jnp.bfloat16)

    def both_ways(to_right, to_left):
        @pl.when(chan < chan_total - 1)
        def _():
            to_right.start()

        @pl.when(chan > 0)
        def _():
            to_left.start()

    def both_land(to_right, to_left):
        @pl.when(chan > 0)
        def _():
            to_right.wait_recv()

        @pl.when(chan < chan_total - 1)
        def _():
            to_left.wait_recv()

    def both_sent(to_right, to_left):
        @pl.when(chan < chan_total - 1)
        def _():
            to_right.wait_send()

        @pl.when(chan > 0)
        def _():
            to_left.wait_send()

    def beside(src, dsts, send, recv):
        return [
            pltpu.make_async_remote_copy(
                src_ref=src, dst_ref=dsts[side], send_sem=send.at[side], recv_sem=recv.at[side],
                device_id=(peer, win), device_id_type=MESH,
            )
            for side, peer in ((0, chan + 1), (1, chan - 1))
        ]

    mean_of = band_mean()
    for copy in small:
        copy.wait()
    fetched[0][0].wait()
    whiten(0, *halves[0])
    pl.semaphore_wait(barrier, 3 + 2 * has_left + 2 * has_right)

    pair_copies = beside(pairs_out, [pair_in.at[0], pair_in.at[1]], pair_send, pair_recv)
    def block_of(p, low, high, sems):
        count = high - low
        return beside(
            near[p].at[pl.ds(chans + low, count)],
            [near[p].at[pl.ds(low, count)], near[p].at[pl.ds(2 * chans + low, count)]],
            part_send.at[sems], part_recv.at[sems],
        )

    part_copies = [block_of(p, 0, chans, p) for p in range(1, len(PARTS))]
    part_copies.insert(0, block_of(0, *halves[1], 0))
    first_copies = block_of(0, *halves[0], len(PARTS))
    both_ways(*first_copies)
    for group in range(GROUPS):
        fetched[group][-1].wait()
        whiten(group, *(halves[1] if group == 0 else (0, chans)))
        rightward = [p for p in TO_RIGHT if PARTS[p][0] == group]
        leftward = [p for p in TO_LEFT if PARTS[p][0] == group]
        for p, q in zip(rightward, leftward):
            both_ways(part_copies[p][0], part_copies[q][1])
        if group == 0:
            both_ways(*pair_copies)
    pass_on = pltpu.make_async_remote_copy(
        src_ref=near[EXTRA].at[pl.ds(0, chans)], dst_ref=beyond.at[pl.ds(0, chans)],
        send_sem=far_send, recv_sem=far_recv, device_id=(chan + 1, win), device_id_type=MESH,
    )
    tables = []
    for group in range(GROUPS):
        for g, quarter in enumerate((win_cross, win_mate, win_across, win)):
            copy = pltpu.make_async_copy(table.at[group, quarter], tab.at[group, g], tab_sem.at[group, g])
            copy.start()
            tables.append(copy)

    both_land(*pair_copies)
    local = pltpu.make_async_copy(pair_in, pair_near, pair_local)
    local.start()
    local.wait()

    empty = 3 * chans
    base = (chan - 1) * chans

    def place(p, carry):
        def put(row, source, receiver, used, low, high):
            at = receiver - base
            fits = (used != 0) & (at >= low) & (at < high)
            src_at[row] = jnp.where(fits, source - base, empty)
            rcv_at[row] = jnp.where(fits, at, empty)

        put(p, pairs[0, p], pairs[1, p], pairs[2, p], 0, 3 * chans)
        at = pairs[1, p] - base
        fits = (pairs[2, p] != 0) & (at >= -chans) & (at < 3 * chans)
        far_src_at[p] = jnp.where(fits, pairs[0, p] - base, empty)
        far_rcv_at[p] = jnp.where(fits & (at >= 0), at, empty)
        beyond_at[p] = jnp.where(fits & (at < 0), at + chans, chans)
        between = has_left * has_right
        put(
            slots + p, pair_near[0, 0, p], pair_near[0, 1, p], pair_near[0, 2, p] * between,
            2 * chans, 3 * chans,
        )
        put(
            2 * slots + p, pair_near[1, 0, p], pair_near[1, 1, p], pair_near[1, 2, p] * between,
            0, chans,
        )
        return carry

    lax.fori_loop(0, slots, place, 0)

    def products(part, low, high, column=0, sources=src_at, receivers=rcv_at, further=None):
        runs = PARTS[part][2]
        half = subs * runs
        here = near[part]
        unroll = 16
        kind = jnp.bfloat16 if half >= 16 else jnp.float32

        def fold(values):
            values = values.astype(jnp.float32).reshape(half // 8, 8, LANES).sum(axis=0)
            count = 8
            while count > runs:
                count //= 2
                values = values[:count] + values[count:]
            return values

        def some(i, carry):
            for j in range(unroll):
                p = low + i * unroll + j
                a = here[sources[p]].astype(kind)
                b = here[receivers[p]].astype(kind)
                if further is not None:
                    b = b + beyond[further[p]].astype(kind)
                real = a[:half] * b[:half] + a[half:] * b[half:]
                imag = a[half:] * b[:half] - a[:half] * b[half:]
                cross[pl.ds(p, runs, stride=pitch), :] = fold(real)
                cross[pl.ds(p + RUNS * pitch, runs, stride=pitch), :] = fold(imag)
            return carry

        lax.fori_loop(0, (high - low) // unroll, some, 0)
        for k in range(2 * runs):
            start = ((k % 2) * RUNS + k // 2) * pitch
            left_rows[low:high, column + k * LANES : column + (k + 1) * LANES] = cross[
                start + low : start + high, :
            ].astype(jnp.bfloat16)

    def lags(low, high, g, group, first, runs):
        depth = 2 * runs * LANES
        return jnp.dot(
            left_rows[low:high, :depth], tab[group, g, 2 * first * LANES : 2 * first * LANES + depth, :],
            preferred_element_type=jnp.float32,
        )

    for copy in tables:
        copy.wait()

    both_land(*first_copies)
    for part in range(LAST):
        both_land(*part_copies[part])
        if part == LAST - 1:
            @pl.when(chan > 0)
            def _():
                part_copies[EXTRA][0].wait_recv()

            @pl.when((chan > 0) & (chan < chan_total - 1))
            def _():
                pass_on.start()

        products(part, 0, rows)
        for g in range(WINS):
            total = lags(0, rows, g, *PARTS[part])
            sums[g] = total if part == 0 else total + sums[g]

    def remote(src, dst, which, peer):
        return pltpu.make_async_remote_copy(
            src_ref=src, dst_ref=dst, send_sem=tail_send.at[which], recv_sem=tail_recv.at[which],
            device_id=peer, device_id_type=MESH,
        )

    both_land(*part_copies[LAST])
    sides = ((0, 2 * slots), (1, slots))

    def kept(low, g, runs):
        return lags(low, low + slots, g, *PARTS[LAST][:2], runs) + sums[g, low : low + slots]

    def to_mate(side, low, runs):
        for g in range(2):
            core_out[side, g] = kept(low, g, runs).astype(jnp.bfloat16)
        copy = remote(core_out.at[side], core_in.at[side], side, (chan, win_mate))
        copy.start()
        return copy

    def to_home(side, ahead, core_copy):
        core_copy.wait_recv()
        copies = []
        for g, to_win in ((0, win_across), (1, win)):
            home_out[side, g] = (ahead[g] + core_in[side, g].astype(jnp.float32)).astype(jnp.bfloat16)
            copies.append(
                remote(home_out.at[side, g], home_in.at[side, g], 2 + 2 * side + g, (chan + 1 - 2 * side, to_win))
            )

        @pl.when(chan < chan_total - 1 if side == 0 else chan > 0)
        def _():
            for copy in copies:
                copy.start()

        return copies

    (_, right_low), (_, left_low) = sides
    alone = PARTS[LAST][2]
    whole = alone + PARTS[EXTRA][2]
    extra_column = 2 * alone * LANES
    products(LAST, right_low, right_low + slots)
    core_right = to_mate(0, right_low, alone)
    ahead = [kept(right_low, 2, alone), kept(right_low, 3, alone)]
    products(LAST, left_low, left_low + slots)
    home_right = to_home(0, ahead, core_right)

    @pl.when(chan < chan_total - 1)
    def _():
        part_copies[EXTRA][1].wait_recv()

    products(EXTRA, left_low, left_low + slots, extra_column)
    core_left = to_mate(1, left_low, whole)
    ahead = [kept(left_low, 2, whole), kept(left_low, 3, whole)]

    products(LAST, 0, slots)
    home_left = to_home(1, ahead, core_left)

    @pl.when(chan >= 2)
    def _():
        pass_on.wait_recv()

    products(EXTRA, 0, slots, extra_column, far_src_at, far_rcv_at, beyond_at)
    own_copies = []
    for g, to_win in ((0, win_cross), (2, win_across), (1, win_mate)):
        own_out[g] = kept(0, g, whole).astype(jnp.bfloat16)
        copy = remote(own_out.at[g], own_in.at[g], 6 + g, (chan, to_win))
        copy.start()
        own_copies.append(copy)
    total = kept(0, 3, whole)

    for copies in part_copies:
        both_sent(*copies)
    both_sent(*first_copies)
    both_sent(*pair_copies)

    @pl.when((chan > 0) & (chan < chan_total - 1))
    def _():
        pass_on.wait_send()

    core_right.wait_send()
    core_left.wait_send()
    for copy in own_copies:
        copy.wait()
    for g in range(3):
        total = total + own_in[g].astype(jnp.float32)
    for to_left in home_left:
        @pl.when(chan < chan_total - 1)
        def _():
            to_left.wait_recv()

        @pl.when(chan > 0)
        def _():
            to_left.wait_send()

    for g in range(2):
        total = total + home_in[1, g].astype(jnp.float32)
    for to_right in home_right:
        @pl.when(chan < chan_total - 1)
        def _():
            to_right.wait_send()

        @pl.when(chan > 0)
        def _():
            to_right.wait_recv()

    for g in range(2):
        total = total + home_in[0, g].astype(jnp.float32)
    out[...] = total


def on_device(chan_total, spectra, pair_list, quality):
    chans, subs = spectra.shape[0], spectra.shape[1]
    slots = pair_list.shape[0]
    rows = 3 * slots
    runs = NF // LANES
    tiles = spectra.reshape(chans, subs, 2, runs, LANES).transpose(0, 1, 3, 2, 4)
    tiles = tiles.reshape(chans, subs, 2 * runs, LANES)
    pairs = pair_list.T
    hbm = pl.BlockSpec(memory_space=pltpu.HBM)
    sem = pltpu.SemaphoreType.DMA
    bf16 = jnp.bfloat16
    total = pl.pallas_call(
        functools.partial(kernel, chan_total),
        out_shape=pltpu.VMEM((slots, WIDE), jnp.float32),
        in_specs=[hbm] * 4,
        out_specs=pl.BlockSpec(memory_space=pltpu.VMEM),
        scratch_shapes=[
            pltpu.VMEM((3 * chans + 1, 2 * subs * part[2], LANES), bf16) for part in PARTS
        ]
        + [
            pltpu.VMEM((chans + 1, 2 * subs * PARTS[EXTRA][2], LANES), bf16),
            pltpu.VMEM((GROUPS, chans, subs, 2 * RUNS, LANES), bf16),
            pltpu.VMEM((4 * subs * RUNS * 2 + 8, LANES), jnp.float32),
            pltpu.VMEM(((2 * RUNS + 1) * (rows + 8), LANES), jnp.float32),
            pltpu.VMEM((rows, 2 * RUNS * LANES), bf16),
            pltpu.VMEM((WINS, rows, WIDE), jnp.float32),
            pltpu.VMEM((GROUPS, WINS, 2 * RUNS * LANES, WIDE), bf16),
            pltpu.SMEM(quality.shape, jnp.int32),
            pltpu.SMEM(pairs.shape, jnp.int32),
            pltpu.VMEM((2,) + pairs.shape, jnp.int32),
            pltpu.SMEM((2,) + pairs.shape, jnp.int32),
            pltpu.SMEM((rows,), jnp.int32),
            pltpu.SMEM((rows,), jnp.int32),
            pltpu.SMEM((slots,), jnp.int32),
            pltpu.SMEM((slots,), jnp.int32),
            pltpu.SMEM((slots,), jnp.int32),
            pltpu.VMEM((2, 2, slots, WIDE), bf16),
            pltpu.VMEM((2, 2, slots, WIDE), bf16),
            pltpu.VMEM((2, 2, slots, WIDE), bf16),
            pltpu.VMEM((2, 2, slots, WIDE), bf16),
            pltpu.VMEM((3, slots, WIDE), bf16),
            pltpu.VMEM((3, slots, WIDE), bf16),
            sem((2,)), sem((GROUPS, 2)), sem((GROUPS, WINS)), sem((len(PARTS) + 1, 2)), sem((len(PARTS) + 1, 2)),
            sem, sem, sem((2,)), sem((2,)), sem, sem((9,)), sem((9,)),
        ],
        compiler_params=pltpu.CompilerParams(
            collective_id=0, has_side_effects=True, vmem_limit_bytes=63 * 1024 * 1024
        ),
    )(quality, pairs, tiles, jnp.asarray(lag_tables()))
    return total * (1.0 / math.sqrt(subs * WINS))


def solution(mesh):
    return jax.shard_map(
        functools.partial(on_device, mesh.shape["chan"]),
        mesh=mesh,
        in_specs=(P("chan", "win", None, None), P("chan", None), P("chan")),
        out_specs=P("chan", "win"),
        check_vma=False,
    )
```

```python
import functools
import math

import jax
import jax.numpy as jnp
import numpy as np
import ml_dtypes
from jax import lax
from jax.experimental import pallas as pl
from jax.experimental.pallas import tpu as pltpu
from jax.sharding import PartitionSpec as P

MESH = pl.DeviceIdType.MESH
NF = 4096
LAGS = 1024
WB = 64
LANES = 128
tiny_level = 1e-06

RUNS = 8
GROUPS = NF // (RUNS * LANES)
PARTS = ((0, 0, 8), (1, 0, 8), (2, 0, 8), (3, 0, 4), (3, 4, 2), (3, 6, 2))
LAST, EXTRA = 4, 5
TO_RIGHT = (0, 1, 2, EXTRA, 3, LAST)
TO_LEFT = (0, 1, 2, 3, LAST, EXTRA)
WINS = 4
WIDE = LAGS // WINS


def lag_tables():
    frequency = np.arange(NF, dtype=np.int64)
    lag_index = np.arange(LAGS, dtype=np.int64) - LAGS // 2
    phase = np.mod(frequency[:, None] * lag_index[None, :], 2 * NF)
    angle = np.arange(2 * NF, dtype=np.float64) * (math.pi / NF)
    scale = 1.0 / math.sqrt(NF)
    cos_of = (np.cos(angle) * scale).astype(ml_dtypes.bfloat16)
    sin_of = (-np.sin(angle) * scale).astype(ml_dtypes.bfloat16)
    both = np.stack([cos_of[phase], sin_of[phase]])
    both = both.reshape(2, GROUPS, RUNS, LANES, WINS, WIDE)
    both = both.transpose(1, 4, 2, 0, 3, 5)
    return both.reshape(GROUPS, WINS, RUNS * 2 * LANES, WIDE)


def band_mean():
    here = lax.broadcasted_iota(jnp.int32, (LANES, LANES), 0) // WB
    there = lax.broadcasted_iota(jnp.int32, (LANES, LANES), 1) // WB
    return jnp.where(here == there, 1.0 / WB, 0.0).astype(jnp.bfloat16)


def kernel(
    chan_total, quality_in, pairs_out, spectra, table,
    out,
    near0, near1, near2, near3, near4, near5, beyond, fresh, loose, cross, left_rows, sums, tab,
    quality, pairs, pair_in, pair_near, src_at, rcv_at, far_src_at, far_rcv_at, beyond_at,
    core_out, core_in, home_out, home_in, own_out, own_in,
    small_sem, fresh_sem, tab_sem, part_send, part_recv, far_send, far_recv, pair_send, pair_recv, pair_local, tail_send, tail_recv,
):
    near = (near0, near1, near2, near3, near4, near5)
    chan = lax.axis_index("chan")
    win = lax.axis_index("win")
    chans = spectra.shape[0]
    subs = spectra.shape[1]
    slots = pairs.shape[1]
    rows = 3 * slots
    pitch = rows + 8
    core = lax.rem(win, 2)
    x_hi = win // 2
    has_left = (chan > 0).astype(jnp.int32)
    has_right = (chan < chan_total - 1).astype(jnp.int32)
    win_mate = x_hi * 2 + 1 - core
    win_across = (1 - x_hi) * 2 + core
    win_cross = (1 - x_hi) * 2 + 1 - core

    barrier = pltpu.get_barrier_semaphore()

    def greet(peer):
        pl.semaphore_signal(barrier, inc=1, device_id=peer, device_id_type=MESH)

    @pl.when(chan < chan_total - 1)
    def _():
        greet((chan + 1, win))
        greet((chan + 1, win_across))

    @pl.when(chan > 0)
    def _():
        greet((chan - 1, win))
        greet((chan - 1, win_across))

    greet((chan, win_mate))
    greet((chan, win_across))
    greet((chan, win_cross))

    small = [
        pltpu.make_async_copy(src, dst, small_sem.at[i])
        for i, (src, dst) in enumerate(((quality_in, quality), (pairs_out, pairs)))
    ]
    for copy in small:
        copy.start()
    halves = [(0, chans // 2), (chans // 2, chans)]
    fetched = []
    for group in range(GROUPS):
        pieces = halves if group == 0 else [(0, chans)]
        copies = []
        for n, (low, high) in enumerate(pieces):
            copy = pltpu.make_async_copy(
                spectra.at[pl.ds(low, high - low), :, pl.ds(group * 2 * RUNS, 2 * RUNS), :],
                fresh.at[group, pl.ds(low, high - low)], fresh_sem.at[group, n],
            )
            copy.start()
            copies.append(copy)
        fetched.append(copies)
    @pl.when(chan == 0)
    def _():
        for part in range(len(PARTS)):
            near[part][0:chans] = jnp.zeros((chans,) + near[part].shape[1:], jnp.bfloat16)
        pair_in[0] = jnp.zeros(pair_in.shape[1:], jnp.int32)
        home_in[0] = jnp.zeros(home_in.shape[1:], jnp.bfloat16)

    beyond[chans] = jnp.zeros(beyond.shape[1:], jnp.bfloat16)

    @pl.when(chan < 2)
    def _():
        beyond[0:chans] = jnp.zeros((chans,) + beyond.shape[1:], jnp.bfloat16)

    @pl.when(chan == chan_total - 1)
    def _():
        for part in range(len(PARTS)):
            near[part][2 * chans : 3 * chans] = jnp.zeros((chans,) + near[part].shape[1:], jnp.bfloat16)
        pair_in[1] = jnp.zeros(pair_in.shape[1:], jnp.int32)
        home_in[1] = jnp.zeros(home_in.shape[1:], jnp.bfloat16)

    def whiten(group, low, high):
        step = 4
        mine = [(p, first, runs) for p, (g, first, runs) in enumerate(PARTS) if g == group]
        def some(i, carry):
            start = low + i * step
            block = fresh[group, pl.ds(start, step)]
            count = step * subs * RUNS
            loose[0 : 2 * count] = block.astype(jnp.float32).reshape(2 * count, LANES)
            real = loose[pl.ds(0, count, stride=2), :]
            imag = loose[pl.ds(1, count, stride=2), :]
            magnitude = jnp.sqrt(real * real + imag * imag)
            level = jnp.dot(magnitude.astype(jnp.bfloat16), mean_of, preferred_element_type=jnp.float32)
            weight = 1.0 / (level + tiny_level)
            real = (real * weight).reshape(step, subs, RUNS, LANES)
            imag = (imag * weight).reshape(step, subs, RUNS, LANES)
            for j in range(step):
                good = quality[start + j].astype(jnp.float32)
                for p, first, runs in mine:
                    kept = [
                        (values[j, :, first : first + runs] * good).reshape(subs * runs, LANES)
                        for values in (real, imag)
                    ]
                    near[p][chans + start + j] = jnp.concatenate(kept, axis=0).astype(jnp.bfloat16)
            return carry

        lax.fori_loop(0, (high - low) // step, some, 0)
        for p, first, runs in mine:
            near[p][3 * chans] = jnp.zeros(near[p].shape[1:], jnp.bfloat16)

    def both_ways(to_right, to_left):
        @pl.when(chan < chan_total - 1)
        def _():
            to_right.start()

        @pl.when(chan > 0)
        def _():
            to_left.start()

    def both_land(to_right, to_left):
        @pl.when(chan > 0)
        def _():
            to_right.wait_recv()

        @pl.when(chan < chan_total - 1)
        def _():
            to_left.wait_recv()

    def both_sent(to_right, to_left):
        @pl.when(chan < chan_total - 1)
        def _():
            to_right.wait_send()

        @pl.when(chan > 0)
        def _():
            to_left.wait_send()

    def beside(src, dsts, send, recv):
        return [
            pltpu.make_async_remote_copy(
                src_ref=src, dst_ref=dsts[side], send_sem=send.at[side], recv_sem=recv.at[side],
                device_id=(peer, win), device_id_type=MESH,
            )
            for side, peer in ((0, chan + 1), (1, chan - 1))
        ]

    mean_of = band_mean()
    for copy in small:
        copy.wait()
    fetched[0][0].wait()
    whiten(0, *halves[0])
    pl.semaphore_wait(barrier, 3 + 2 * has_left + 2 * has_right)

    pair_copies = beside(pairs_out, [pair_in.at[0], pair_in.at[1]], pair_send, pair_recv)
    def block_of(p, low, high, sems):
        count = high - low
        return beside(
            near[p].at[pl.ds(chans + low, count)],
            [near[p].at[pl.ds(low, count)], near[p].at[pl.ds(2 * chans + low, count)]],
            part_send.at[sems], part_recv.at[sems],
        )

    part_copies = [block_of(p, 0, chans, p) for p in range(1, len(PARTS))]
    part_copies.insert(0, block_of(0, *halves[1], 0))
    first_copies = block_of(0, *halves[0], len(PARTS))
    both_ways(*first_copies)
    for group in range(GROUPS):
        fetched[group][-1].wait()
        whiten(group, *(halves[1] if group == 0 else (0, chans)))
        rightward = [p for p in TO_RIGHT if PARTS[p][0] == group]
        leftward = [p for p in TO_LEFT if PARTS[p][0] == group]
        for p, q in zip(rightward, leftward):
            both_ways(part_copies[p][0], part_copies[q][1])
        if group == 0:
            both_ways(*pair_copies)
    pass_on = pltpu.make_async_remote_copy(
        src_ref=near[EXTRA].at[pl.ds(0, chans)], dst_ref=beyond.at[pl.ds(0, chans)],
        send_sem=far_send, recv_sem=far_recv, device_id=(chan + 1, win), device_id_type=MESH,
    )
    tables = []
    for group in range(GROUPS):
        for g, quarter in enumerate((win_cross, win_mate, win_across, win)):
            copy = pltpu.make_async_copy(table.at[group, quarter], tab.at[group, g], tab_sem.at[group, g])
            copy.start()
            tables.append(copy)

    both_land(*pair_copies)
    local = pltpu.make_async_copy(pair_in, pair_near, pair_local)
    local.start()
    local.wait()

    empty = 3 * chans
    base = (chan - 1) * chans

    def place(p, carry):
        def put(row, source, receiver, used, low, high):
            at = receiver - base
            fits = (used != 0) & (at >= low) & (at < high)
            src_at[row] = jnp.where(fits, source - base, empty)
            rcv_at[row] = jnp.where(fits, at, empty)

        put(p, pairs[0, p], pairs[1, p], pairs[2, p], 0, 3 * chans)
        at = pairs[1, p] - base
        fits = (pairs[2, p] != 0) & (at >= -chans) & (at < 3 * chans)
        far_src_at[p] = jnp.where(fits, pairs[0, p] - base, empty)
        far_rcv_at[p] = jnp.where(fits & (at >= 0), at, empty)
        beyond_at[p] = jnp.where(fits & (at < 0), at + chans, chans)
        between = has_left * has_right
        put(
            slots + p, pair_near[0, 0, p], pair_near[0, 1, p], pair_near[0, 2, p] * between,
            2 * chans, 3 * chans,
        )
        put(
            2 * slots + p, pair_near[1, 0, p], pair_near[1, 1, p], pair_near[1, 2, p] * between,
            0, chans,
        )
        return carry

    lax.fori_loop(0, slots, place, 0)

    def products(part, low, high, column=0, sources=src_at, receivers=rcv_at, further=None):
        runs = PARTS[part][2]
        half = subs * runs
        here = near[part]
        unroll = 16
        kind = jnp.bfloat16 if half >= 16 else jnp.float32

        def fold(values):
            values = values.astype(jnp.float32).reshape(half // 8, 8, LANES).sum(axis=0)
            count = 8
            while count > runs:
                count //= 2
                values = values[:count] + values[count:]
            return values

        def some(i, carry):
            for j in range(unroll):
                p = low + i * unroll + j
                a = here[sources[p]].astype(kind)
                b = here[receivers[p]].astype(kind)
                if further is not None:
                    b = b + beyond[further[p]].astype(kind)
                real = a[:half] * b[:half] + a[half:] * b[half:]
                imag = a[half:] * b[:half] - a[:half] * b[half:]
                cross[pl.ds(p, runs, stride=pitch), :] = fold(real)
                cross[pl.ds(p + RUNS * pitch, runs, stride=pitch), :] = fold(imag)
            return carry

        lax.fori_loop(0, (high - low) // unroll, some, 0)
        for k in range(2 * runs):
            start = ((k % 2) * RUNS + k // 2) * pitch
            left_rows[low:high, column + k * LANES : column + (k + 1) * LANES] = cross[
                start + low : start + high, :
            ].astype(jnp.bfloat16)

    def lags(low, high, g, group, first, runs):
        depth = 2 * runs * LANES
        return jnp.dot(
            left_rows[low:high, :depth], tab[group, g, 2 * first * LANES : 2 * first * LANES + depth, :],
            preferred_element_type=jnp.float32,
        )

    for copy in tables:
        copy.wait()

    both_land(*first_copies)
    for part in range(LAST):
        both_land(*part_copies[part])
        if part == LAST - 1:
            @pl.when(chan > 0)
            def _():
                part_copies[EXTRA][0].wait_recv()

            @pl.when((chan > 0) & (chan < chan_total - 1))
            def _():
                pass_on.start()

        products(part, 0, rows)
        for g in range(WINS):
            total = lags(0, rows, g, *PARTS[part])
            sums[g] = total if part == 0 else total + sums[g]

    def remote(src, dst, which, peer):
        return pltpu.make_async_remote_copy(
            src_ref=src, dst_ref=dst, send_sem=tail_send.at[which], recv_sem=tail_recv.at[which],
            device_id=peer, device_id_type=MESH,
        )

    both_land(*part_copies[LAST])
    sides = ((0, 2 * slots), (1, slots))

    def kept(low, g, runs, part=LAST):
        return lags(low, low + slots, g, *PARTS[part][:2], runs) + sums[g, low : low + slots]

    def to_mate(side, low, runs):
        copies = []
        for g in range(2):
            core_out[side, g] = kept(low, g, runs).astype(jnp.bfloat16)
            copy = remote(core_out.at[side, g], core_in.at[side, g], 2 * side + g, (chan, win_mate))
            copy.start()
            copies.append(copy)
        return copies

    def to_home(side, ahead, core_copies):
        copies = []
        for g, to_win in ((0, win_across), (1, win)):
            core_copies[g].wait_recv()
            home_out[side, g] = (ahead[g] + core_in[side, g].astype(jnp.float32)).astype(jnp.bfloat16)
            copy = remote(
                home_out.at[side, g], home_in.at[side, g], 4 + 2 * side + g, (chan + 1 - 2 * side, to_win)
            )
            copies.append(copy)

            @pl.when(chan < chan_total - 1 if side == 0 else chan > 0)
            def _():
                copy.start()

        return copies

    (_, right_low), (_, left_low) = sides
    alone = PARTS[LAST][2]
    whole = alone + PARTS[EXTRA][2]
    extra_column = 2 * alone * LANES
    products(LAST, right_low, right_low + slots)
    core_right = to_mate(0, right_low, alone)
    ahead = [kept(right_low, 2, alone), kept(right_low, 3, alone)]
    products(LAST, left_low, left_low + slots)
    home_right = to_home(0, ahead, core_right)

    @pl.when(chan < chan_total - 1)
    def _():
        part_copies[EXTRA][1].wait_recv()

    products(EXTRA, left_low, left_low + slots, extra_column)
    core_left = to_mate(1, left_low, whole)
    ahead = [kept(left_low, 2, whole), kept(left_low, 3, whole)]

    products(LAST, 0, slots)
    home_left = to_home(1, ahead, core_left)
    for g in range(WINS):
        sums[g, 0:slots] = kept(0, g, alone)

    @pl.when(chan >= 2)
    def _():
        pass_on.wait_recv()

    products(EXTRA, 0, slots, 0, far_src_at, far_rcv_at, beyond_at)
    own_copies = []
    for g, to_win in ((0, win_cross), (2, win_across), (1, win_mate)):
        own_out[g] = kept(0, g, PARTS[EXTRA][2], EXTRA).astype(jnp.bfloat16)
        copy = remote(own_out.at[g], own_in.at[g], 8 + g, (chan, to_win))
        copy.start()
        own_copies.append(copy)
    total = kept(0, 3, PARTS[EXTRA][2], EXTRA)

    for copies in part_copies:
        both_sent(*copies)
    both_sent(*first_copies)
    both_sent(*pair_copies)

    @pl.when((chan > 0) & (chan < chan_total - 1))
    def _():
        pass_on.wait_send()

    for copy in core_right + core_left:
        copy.wait_send()
    for copy in own_copies:
        copy.wait()
    for g in range(3):
        total = total + own_in[g].astype(jnp.float32)
    for to_left in home_left:
        @pl.when(chan < chan_total - 1)
        def _():
            to_left.wait_recv()

        @pl.when(chan > 0)
        def _():
            to_left.wait_send()

    for g in range(2):
        total = total + home_in[1, g].astype(jnp.float32)
    for to_right in home_right:
        @pl.when(chan < chan_total - 1)
        def _():
            to_right.wait_send()

        @pl.when(chan > 0)
        def _():
            to_right.wait_recv()

    for g in range(2):
        total = total + home_in[0, g].astype(jnp.float32)
    out[...] = total


def on_device(chan_total, spectra, pair_list, quality):
    chans, subs = spectra.shape[0], spectra.shape[1]
    slots = pair_list.shape[0]
    rows = 3 * slots
    runs = NF // LANES
    tiles = spectra.reshape(chans, subs, 2, runs, LANES).transpose(0, 1, 3, 2, 4)
    tiles = tiles.reshape(chans, subs, 2 * runs, LANES)
    pairs = pair_list.T
    hbm = pl.BlockSpec(memory_space=pltpu.HBM)
    sem = pltpu.SemaphoreType.DMA
    bf16 = jnp.bfloat16
    total = pl.pallas_call(
        functools.partial(kernel, chan_total),
        out_shape=pltpu.VMEM((slots, WIDE), jnp.float32),
        in_specs=[hbm] * 4,
        out_specs=pl.BlockSpec(memory_space=pltpu.VMEM),
        scratch_shapes=[
            pltpu.VMEM((3 * chans + 1, 2 * subs * part[2], LANES), bf16) for part in PARTS
        ]
        + [
            pltpu.VMEM((chans + 1, 2 * subs * PARTS[EXTRA][2], LANES), bf16),
            pltpu.VMEM((GROUPS, chans, subs, 2 * RUNS, LANES), bf16),
            pltpu.VMEM((4 * subs * RUNS * 2 + 8, LANES), jnp.float32),
            pltpu.VMEM(((2 * RUNS + 1) * (rows + 8), LANES), jnp.float32),
            pltpu.VMEM((rows, 2 * RUNS * LANES), bf16),
            pltpu.VMEM((WINS, rows, WIDE), jnp.float32),
            pltpu.VMEM((GROUPS, WINS, 2 * RUNS * LANES, WIDE), bf16),
            pltpu.SMEM(quality.shape, jnp.int32),
            pltpu.SMEM(pairs.shape, jnp.int32),
            pltpu.VMEM((2,) + pairs.shape, jnp.int32),
            pltpu.SMEM((2,) + pairs.shape, jnp.int32),
            pltpu.SMEM((rows,), jnp.int32),
            pltpu.SMEM((rows,), jnp.int32),
            pltpu.SMEM((slots,), jnp.int32),
            pltpu.SMEM((slots,), jnp.int32),
            pltpu.SMEM((slots,), jnp.int32),
            pltpu.VMEM((2, 2, slots, WIDE), bf16),
            pltpu.VMEM((2, 2, slots, WIDE), bf16),
            pltpu.VMEM((2, 2, slots, WIDE), bf16),
            pltpu.VMEM((2, 2, slots, WIDE), bf16),
            pltpu.VMEM((3, slots, WIDE), bf16),
            pltpu.VMEM((3, slots, WIDE), bf16),
            sem((2,)), sem((GROUPS, 2)), sem((GROUPS, WINS)), sem((len(PARTS) + 1, 2)), sem((len(PARTS) + 1, 2)),
            sem, sem, sem((2,)), sem((2,)), sem, sem((11,)), sem((11,)),
        ],
        compiler_params=pltpu.CompilerParams(
            collective_id=0, has_side_effects=True, vmem_limit_bytes=63 * 1024 * 1024
        ),
    )(quality, pairs, tiles, jnp.asarray(lag_tables()))
    return total * (1.0 / math.sqrt(subs * WINS))


def solution(mesh):
    return jax.shard_map(
        functools.partial(on_device, mesh.shape["chan"]),
        mesh=mesh,
        in_specs=(P("chan", "win", None, None), P("chan", None), P("chan")),
        out_specs=P("chan", "win"),
        check_vma=False,
    )
```

```python
import functools
import math

import jax
import jax.numpy as jnp
import numpy as np
import ml_dtypes
from jax import lax
from jax.experimental import pallas as pl
from jax.experimental.pallas import tpu as pltpu
from jax.sharding import PartitionSpec as P

MESH = pl.DeviceIdType.MESH
NF = 4096
LAGS = 1024
WB = 64
LANES = 128
tiny_level = 1e-06

RUNS = 8
GROUPS = NF // (RUNS * LANES)
PARTS = ((0, 0, 8), (1, 0, 8), (2, 0, 8), (3, 0, 4), (3, 4, 2), (3, 6, 2))
LAST, EXTRA = 4, 5
TO_RIGHT = (0, 1, 2, EXTRA, 3, LAST)
TO_LEFT = (0, 1, 2, 3, LAST, EXTRA)
WINS = 4
WIDE = LAGS // WINS


def lag_tables():
    frequency = np.arange(NF, dtype=np.int64)
    lag_index = np.arange(LAGS, dtype=np.int64) - LAGS // 2
    phase = np.mod(frequency[:, None] * lag_index[None, :], 2 * NF)
    angle = np.arange(2 * NF, dtype=np.float64) * (math.pi / NF)
    scale = 1.0 / math.sqrt(NF)
    cos_of = (np.cos(angle) * scale).astype(ml_dtypes.bfloat16)
    sin_of = (-np.sin(angle) * scale).astype(ml_dtypes.bfloat16)
    both = np.stack([cos_of[phase], sin_of[phase]])
    both = both.reshape(2, GROUPS, RUNS, LANES, WINS, WIDE)
    both = both.transpose(1, 4, 2, 0, 3, 5)
    return both.reshape(GROUPS, WINS, RUNS * 2 * LANES, WIDE)


def band_mean():
    here = lax.broadcasted_iota(jnp.int32, (LANES, LANES), 0) // WB
    there = lax.broadcasted_iota(jnp.int32, (LANES, LANES), 1) // WB
    return jnp.where(here == there, 1.0 / WB, 0.0).astype(jnp.bfloat16)


def kernel(
    chan_total, quality_in, pairs_out, spectra, table,
    out,
    near0, near1, near2, near3, near4, near5, beyond, fresh, loose, cross, left_rows, sums, tab,
    quality, pairs, pair_in, pair_near, src_at, rcv_at, far_src_at, far_rcv_at, beyond_at,
    core_out, core_in, home_out, home_in, own_out, own_in,
    small_sem, fresh_sem, tab_sem, part_send, part_recv, far_send, far_recv, pair_send, pair_recv, pair_local, tail_send, tail_recv,
):
    near = (near0, near1, near2, near3, near4, near5)
    chan = lax.axis_index("chan")
    win = lax.axis_index("win")
    chans = spectra.shape[0]
    subs = spectra.shape[1]
    slots = pairs.shape[1]
    rows = 3 * slots
    pitch = rows + 8
    core = lax.rem(win, 2)
    x_hi = win // 2
    has_left = (chan > 0).astype(jnp.int32)
    has_right = (chan < chan_total - 1).astype(jnp.int32)
    win_mate = x_hi * 2 + 1 - core
    win_across = (1 - x_hi) * 2 + core
    win_cross = (1 - x_hi) * 2 + 1 - core

    barrier = pltpu.get_barrier_semaphore()

    def greet(peer):
        pl.semaphore_signal(barrier, inc=1, device_id=peer, device_id_type=MESH)

    @pl.when(chan < chan_total - 1)
    def _():
        greet((chan + 1, win))
        greet((chan + 1, win_across))

    @pl.when(chan > 0)
    def _():
        greet((chan - 1, win))
        greet((chan - 1, win_across))

    greet((chan, win_mate))
    greet((chan, win_across))
    greet((chan, win_cross))

    small = [
        pltpu.make_async_copy(src, dst, small_sem.at[i])
        for i, (src, dst) in enumerate(((quality_in, quality), (pairs_out, pairs)))
    ]
    for copy in small:
        copy.start()
    halves = [(0, chans // 2), (chans // 2, chans)]
    fetched = []
    for group in range(GROUPS):
        pieces = halves if group == 0 else [(0, chans)]
        copies = []
        for n, (low, high) in enumerate(pieces):
            copy = pltpu.make_async_copy(
                spectra.at[pl.ds(low, high - low), :, pl.ds(group * 2 * RUNS, 2 * RUNS), :],
                fresh.at[group, pl.ds(low, high - low)], fresh_sem.at[group, n],
            )
            copy.start()
            copies.append(copy)
        fetched.append(copies)
    @pl.when(chan == 0)
    def _():
        for part in range(len(PARTS)):
            near[part][0:chans] = jnp.zeros((chans,) + near[part].shape[1:], jnp.bfloat16)
        pair_in[0] = jnp.zeros(pair_in.shape[1:], jnp.int32)
        home_in[0] = jnp.zeros(home_in.shape[1:], jnp.bfloat16)

    beyond[chans] = jnp.zeros(beyond.shape[1:], jnp.bfloat16)

    @pl.when(chan < 2)
    def _():
        beyond[0:chans] = jnp.zeros((chans,) + beyond.shape[1:], jnp.bfloat16)

    @pl.when(chan == chan_total - 1)
    def _():
        for part in range(len(PARTS)):
            near[part][2 * chans : 3 * chans] = jnp.zeros((chans,) + near[part].shape[1:], jnp.bfloat16)
        pair_in[1] = jnp.zeros(pair_in.shape[1:], jnp.int32)
        home_in[1] = jnp.zeros(home_in.shape[1:], jnp.bfloat16)

    def whiten(group, low, high):
        step = 4
        mine = [(p, first, runs) for p, (g, first, runs) in enumerate(PARTS) if g == group]
        def some(i, carry):
            start = low + i * step
            block = fresh[group, pl.ds(start, step)]
            count = step * subs * RUNS
            loose[0 : 2 * count] = block.astype(jnp.float32).reshape(2 * count, LANES)
            real = loose[pl.ds(0, count, stride=2), :]
            imag = loose[pl.ds(1, count, stride=2), :]
            magnitude = jnp.sqrt(real * real + imag * imag)
            level = jnp.dot(magnitude.astype(jnp.bfloat16), mean_of, preferred_element_type=jnp.float32)
            weight = 1.0 / (level + tiny_level)
            real = (real * weight).reshape(step, subs, RUNS, LANES)
            imag = (imag * weight).reshape(step, subs, RUNS, LANES)
            for j in range(step):
                good = quality[start + j].astype(jnp.float32)
                for p, first, runs in mine:
                    kept = [
                        (values[j, :, first : first + runs] * good).reshape(subs * runs, LANES)
                        for values in (real, imag)
                    ]
                    near[p][chans + start + j] = jnp.concatenate(kept, axis=0).astype(jnp.bfloat16)
            return carry

        lax.fori_loop(0, (high - low) // step, some, 0)
        for p, first, runs in mine:
            near[p][3 * chans] = jnp.zeros(near[p].shape[1:], jnp.bfloat16)

    def both_ways(to_right, to_left):
        @pl.when(chan < chan_total - 1)
        def _():
            to_right.start()

        @pl.when(chan > 0)
        def _():
            to_left.start()

    def both_land(to_right, to_left):
        @pl.when(chan > 0)
        def _():
            to_right.wait_recv()

        @pl.when(chan < chan_total - 1)
        def _():
            to_left.wait_recv()

    def both_sent(to_right, to_left):
        @pl.when(chan < chan_total - 1)
        def _():
            to_right.wait_send()

        @pl.when(chan > 0)
        def _():
            to_left.wait_send()

    def beside(src, dsts, send, recv):
        return [
            pltpu.make_async_remote_copy(
                src_ref=src, dst_ref=dsts[side], send_sem=send.at[side], recv_sem=recv.at[side],
                device_id=(peer, win), device_id_type=MESH,
            )
            for side, peer in ((0, chan + 1), (1, chan - 1))
        ]

    mean_of = band_mean()
    for copy in small:
        copy.wait()
    fetched[0][0].wait()
    whiten(0, *halves[0])
    pl.semaphore_wait(barrier, 3 + 2 * has_left + 2 * has_right)

    pair_copies = beside(pairs_out, [pair_in.at[0], pair_in.at[1]], pair_send, pair_recv)
    def block_of(p, low, high, sems):
        count = high - low
        return beside(
            near[p].at[pl.ds(chans + low, count)],
            [near[p].at[pl.ds(low, count)], near[p].at[pl.ds(2 * chans + low, count)]],
            part_send.at[sems], part_recv.at[sems],
        )

    part_copies = [block_of(p, 0, chans, p) for p in range(1, len(PARTS))]
    part_copies.insert(0, block_of(0, *halves[1], 0))
    first_copies = block_of(0, *halves[0], len(PARTS))
    both_ways(*first_copies)
    for group in range(GROUPS):
        fetched[group][-1].wait()
        whiten(group, *(halves[1] if group == 0 else (0, chans)))
        rightward = [p for p in TO_RIGHT if PARTS[p][0] == group]
        leftward = [p for p in TO_LEFT if PARTS[p][0] == group]
        for p, q in zip(rightward, leftward):
            both_ways(part_copies[p][0], part_copies[q][1])
        if group == 0:
            both_ways(*pair_copies)
    pass_on = pltpu.make_async_remote_copy(
        src_ref=near[EXTRA].at[pl.ds(0, chans)], dst_ref=beyond.at[pl.ds(0, chans)],
        send_sem=far_send, recv_sem=far_recv, device_id=(chan + 1, win), device_id_type=MESH,
    )
    tables = []
    for group in range(GROUPS):
        for g, quarter in enumerate((win_cross, win_mate, win_across, win)):
            copy = pltpu.make_async_copy(table.at[group, quarter], tab.at[group, g], tab_sem.at[group, g])
            copy.start()
            tables.append(copy)

    both_land(*pair_copies)
    local = pltpu.make_async_copy(pair_in, pair_near, pair_local)
    local.start()
    local.wait()

    empty = 3 * chans
    base = (chan - 1) * chans

    def place(p, carry):
        def put(row, source, receiver, used, low, high):
            at = receiver - base
            fits = (used != 0) & (at >= low) & (at < high)
            src_at[row] = jnp.where(fits, source - base, empty)
            rcv_at[row] = jnp.where(fits, at, empty)

        put(p, pairs[0, p], pairs[1, p], pairs[2, p], 0, 3 * chans)
        at = pairs[1, p] - base
        fits = (pairs[2, p] != 0) & (at >= -chans) & (at < 3 * chans)
        far_src_at[p] = jnp.where(fits, pairs[0, p] - base, empty)
        far_rcv_at[p] = jnp.where(fits & (at >= 0), at, empty)
        beyond_at[p] = jnp.where(fits & (at < 0), at + chans, chans)
        between = has_left * has_right
        put(
            slots + p, pair_near[0, 0, p], pair_near[0, 1, p], pair_near[0, 2, p] * between,
            2 * chans, 3 * chans,
        )
        put(
            2 * slots + p, pair_near[1, 0, p], pair_near[1, 1, p], pair_near[1, 2, p] * between,
            0, chans,
        )
        return carry

    lax.fori_loop(0, slots, place, 0)

    def products(part, low, high, column=0, sources=src_at, receivers=rcv_at, further=None):
        runs = PARTS[part][2]
        half = subs * runs
        here = near[part]
        unroll = 16
        kind = jnp.bfloat16 if half >= 16 else jnp.float32

        def fold(values):
            values = values.astype(jnp.float32).reshape(half // 8, 8, LANES).sum(axis=0)
            count = 8
            while count > runs:
                count //= 2
                values = values[:count] + values[count:]
            return values

        def some(i, carry):
            for j in range(unroll):
                p = low + i * unroll + j
                a = here[sources[p]].astype(kind)
                b = here[receivers[p]].astype(kind)
                if further is not None:
                    b = b + beyond[further[p]].astype(kind)
                real = a[:half] * b[:half] + a[half:] * b[half:]
                imag = a[half:] * b[:half] - a[:half] * b[half:]
                cross[pl.ds(p, runs, stride=pitch), :] = fold(real)
                cross[pl.ds(p + RUNS * pitch, runs, stride=pitch), :] = fold(imag)
            return carry

        lax.fori_loop(0, (high - low) // unroll, some, 0)
        for k in range(2 * runs):
            start = ((k % 2) * RUNS + k // 2) * pitch
            left_rows[low:high, column + k * LANES : column + (k + 1) * LANES] = cross[
                start + low : start + high, :
            ].astype(jnp.bfloat16)

    def lags(low, high, g, group, first, runs):
        depth = 2 * runs * LANES
        return jnp.dot(
            left_rows[low:high, :depth], tab[group, g, 2 * first * LANES : 2 * first * LANES + depth, :],
            preferred_element_type=jnp.float32,
        )

    for copy in tables:
        copy.wait()

    both_land(*first_copies)
    for part in range(LAST):
        both_land(*part_copies[part])
        if part == LAST - 1:
            @pl.when(chan > 0)
            def _():
                part_copies[EXTRA][0].wait_recv()

            @pl.when((chan > 0) & (chan < chan_total - 1))
            def _():
                pass_on.start()

        products(part, 0, rows)
        for g in range(WINS):
            total = lags(0, rows, g, *PARTS[part])
            sums[g] = total if part == 0 else total + sums[g]

    def remote(src, dst, which, peer):
        return pltpu.make_async_remote_copy(
            src_ref=src, dst_ref=dst, send_sem=tail_send.at[which], recv_sem=tail_recv.at[which],
            device_id=peer, device_id_type=MESH,
        )

    both_land(*part_copies[LAST])
    sides = ((0, 2 * slots), (1, slots))

    def kept(low, g, runs, part=LAST):
        return lags(low, low + slots, g, *PARTS[part][:2], runs) + sums[g, low : low + slots]

    def to_mate(side, low, runs):
        for g in range(2):
            core_out[side, g] = kept(low, g, runs).astype(jnp.bfloat16)
        copy = remote(core_out.at[side], core_in.at[side], side, (chan, win_mate))
        copy.start()
        return copy

    def to_home(side, ahead, core_copy):
        core_copy.wait_recv()
        copies = []
        for g, to_win in ((0, win_across), (1, win)):
            home_out[side, g] = (ahead[g] + core_in[side, g].astype(jnp.float32)).astype(jnp.bfloat16)
            copies.append(
                remote(home_out.at[side, g], home_in.at[side, g], 2 + 2 * side + g, (chan + 1 - 2 * side, to_win))
            )

        @pl.when(chan < chan_total - 1 if side == 0 else chan > 0)
        def _():
            for copy in copies:
                copy.start()

        return copies

    (_, right_low), (_, left_low) = sides
    alone = PARTS[LAST][2]
    whole = alone + PARTS[EXTRA][2]
    extra_column = 2 * alone * LANES
    products(LAST, right_low, right_low + slots)
    core_right = to_mate(0, right_low, alone)
    ahead = [kept(right_low, 2, alone), kept(right_low, 3, alone)]
    products(LAST, left_low, left_low + slots)
    home_right = to_home(0, ahead, core_right)

    @pl.when(chan < chan_total - 1)
    def _():
        part_copies[EXTRA][1].wait_recv()

    products(EXTRA, left_low, left_low + slots, extra_column)
    core_left = to_mate(1, left_low, whole)
    ahead = [kept(left_low, 2, whole), kept(left_low, 3, whole)]

    products(LAST, 0, slots)
    home_left = to_home(1, ahead, core_left)
    for g in range(WINS):
        sums[g, 0:slots] = kept(0, g, alone)

    @pl.when(chan >= 2)
    def _():
        pass_on.wait_recv()

    products(EXTRA, 0, slots, 0, far_src_at, far_rcv_at, beyond_at)
    own_copies = []
    for g, to_win in ((0, win_cross), (2, win_across), (1, win_mate)):
        own_out[g] = kept(0, g, PARTS[EXTRA][2], EXTRA).astype(jnp.bfloat16)
        copy = remote(own_out.at[g], own_in.at[g], 6 + g, (chan, to_win))
        copy.start()
        own_copies.append(copy)
    total = kept(0, 3, PARTS[EXTRA][2], EXTRA)

    for copies in part_copies:
        both_sent(*copies)
    both_sent(*first_copies)
    both_sent(*pair_copies)

    @pl.when((chan > 0) & (chan < chan_total - 1))
    def _():
        pass_on.wait_send()

    core_right.wait_send()
    core_left.wait_send()
    for copy in own_copies:
        copy.wait()
    for g in range(3):
        total = total + own_in[g].astype(jnp.float32)
    for to_left in home_left:
        @pl.when(chan < chan_total - 1)
        def _():
            to_left.wait_recv()

        @pl.when(chan > 0)
        def _():
            to_left.wait_send()

    for g in range(2):
        total = total + home_in[1, g].astype(jnp.float32)
    for to_right in home_right:
        @pl.when(chan < chan_total - 1)
        def _():
            to_right.wait_send()

        @pl.when(chan > 0)
        def _():
            to_right.wait_recv()

    for g in range(2):
        total = total + home_in[0, g].astype(jnp.float32)
    out[...] = total


def on_device(chan_total, spectra, pair_list, quality):
    chans, subs = spectra.shape[0], spectra.shape[1]
    slots = pair_list.shape[0]
    rows = 3 * slots
    runs = NF // LANES
    tiles = spectra.reshape(chans, subs, 2, runs, LANES).transpose(0, 1, 3, 2, 4)
    tiles = tiles.reshape(chans, subs, 2 * runs, LANES)
    pairs = pair_list.T
    hbm = pl.BlockSpec(memory_space=pltpu.HBM)
    sem = pltpu.SemaphoreType.DMA
    bf16 = jnp.bfloat16
    total = pl.pallas_call(
        functools.partial(kernel, chan_total),
        out_shape=pltpu.VMEM((slots, WIDE), jnp.float32),
        in_specs=[hbm] * 4,
        out_specs=pl.BlockSpec(memory_space=pltpu.VMEM),
        scratch_shapes=[
            pltpu.VMEM((3 * chans + 1, 2 * subs * part[2], LANES), bf16) for part in PARTS
        ]
        + [
            pltpu.VMEM((chans + 1, 2 * subs * PARTS[EXTRA][2], LANES), bf16),
            pltpu.VMEM((GROUPS, chans, subs, 2 * RUNS, LANES), bf16),
            pltpu.VMEM((4 * subs * RUNS * 2 + 8, LANES), jnp.float32),
            pltpu.VMEM(((2 * RUNS + 1) * (rows + 8), LANES), jnp.float32),
            pltpu.VMEM((rows, 2 * RUNS * LANES), bf16),
            pltpu.VMEM((WINS, rows, WIDE), jnp.float32),
            pltpu.VMEM((GROUPS, WINS, 2 * RUNS * LANES, WIDE), bf16),
            pltpu.SMEM(quality.shape, jnp.int32),
            pltpu.SMEM(pairs.shape, jnp.int32),
            pltpu.VMEM((2,) + pairs.shape, jnp.int32),
            pltpu.SMEM((2,) + pairs.shape, jnp.int32),
            pltpu.SMEM((rows,), jnp.int32),
            pltpu.SMEM((rows,), jnp.int32),
            pltpu.SMEM((slots,), jnp.int32),
            pltpu.SMEM((slots,), jnp.int32),
            pltpu.SMEM((slots,), jnp.int32),
            pltpu.VMEM((2, 2, slots, WIDE), bf16),
            pltpu.VMEM((2, 2, slots, WIDE), bf16),
            pltpu.VMEM((2, 2, slots, WIDE), bf16),
            pltpu.VMEM((2, 2, slots, WIDE), bf16),
            pltpu.VMEM((3, slots, WIDE), bf16),
            pltpu.VMEM((3, slots, WIDE), bf16),
            sem((2,)), sem((GROUPS, 2)), sem((GROUPS, WINS)), sem((len(PARTS) + 1, 2)), sem((len(PARTS) + 1, 2)),
            sem, sem, sem((2,)), sem((2,)), sem, sem((9,)), sem((9,)),
        ],
        compiler_params=pltpu.CompilerParams(
            collective_id=0, has_side_effects=True, vmem_limit_bytes=63 * 1024 * 1024
        ),
    )(quality, pairs, tiles, jnp.asarray(lag_tables()))
    return total * (1.0 / math.sqrt(subs * WINS))


def solution(mesh):
    return jax.shard_map(
        functools.partial(on_device, mesh.shape["chan"]),
        mesh=mesh,
        in_specs=(P("chan", "win", None, None), P("chan", None), P("chan")),
        out_specs=P("chan", "win"),
        check_vma=False,
    )
```
